32 devices in a mesh: seq: 8 (over z, x), tp: 4 (over y, core).
Axes of the slice: x: 2, y: 2, z: 4, core: 2. Of those that a mesh axis runs over, the one named last changes fastest.
Arguments:
- hidden_in: bfloat16 [4096, 2048], P(('seq', 'tp')), may hold values from -6 to 6
- lengths: int32 [8], replicated, may hold values from 1 to 3869, as said below
- ln1_gain: float32 [2048], replicated, may hold values from 0.25 to 1.75
- ln1_bias: float32 [2048], replicated, may hold values from -3 to 3
- w_query: bfloat16 [2048, 2048], P(None, 'tp'), may hold values from -0.125 to 0.125
- b_query: float32 [2048], P('tp'), may hold values from -3 to 3
- w_kv: bfloat16 [2048, 256], replicated, may hold values from -0.125 to 0.125
- b_value: float32 [128], replicated, may hold values from -0.12 to 0.12
- w_out: bfloat16 [2048, 2048], P('tp'), may hold values from -3 to 3
- b_out: float32 [2048], replicated, may hold values from -3 to 3
- ln2_gain: float32 [2048], replicated, may hold values from 0.25 to 1.75
- ln2_bias: float32 [2048], replicated, may hold values from -3 to 3
- w_fc: bfloat16 [2048, 8192], P(None, 'tp'), may hold values from -0.125 to 0.125
- b_fc: float32 [8192], P('tp'), may hold values from -3 to 3
- w_proj: bfloat16 [8192, 2048], P('tp'), may hold values from -0.0625 to 0.0625
- b_proj: float32 [2048], replicated, may hold values from -3 to 3
- grad_out: bfloat16 [4096, 2048], P(('seq', 'tp')), may hold values from -6 to 6
Outputs:
- layer_out: bfloat16 [4096, 2048], P(('seq', 'tp'))
- grad_in: float32 [4096, 2048], P(('seq', 'tp'))
- grad_ln1_gain: float32 [2048], replicated
- grad_ln1_bias: float32 [2048], replicated
- grad_w_query: float32 [2048, 2048], P('seq', 'tp')
- grad_b_query: float32 [2048], P('tp')
- grad_w_kv: float32 [2048, 256], replicated
- grad_b_value: float32 [128], replicated
- grad_w_out: float32 [2048, 2048], P('tp', 'seq')
- grad_b_out: float32 [2048], replicated
- grad_ln2_gain: float32 [2048], replicated
- grad_ln2_bias: float32 [2048], replicated
- grad_w_fc: float32 [2048, 8192], P('seq', 'tp')
- grad_b_fc: float32 [8192], P('tp')
- grad_w_proj: float32 [8192, 2048], P('tp', 'seq')
- grad_b_proj: float32 [2048], replicated
The draws below stay inside these ranges and needn't reach their ends.
Inputs may be any that keep to these rules, and one draw needn't show every extreme that they name: The 8 document lengths of the window, in order, sum to 4096. All but one are short, at most max(1, 64); they come in pairs whose two lengths add to max(1, 64) + 1, with one more of (max(1, 64) + 1) // 2 when (7) is odd, in an order drawn from the seed. The remaining one, at a place drawn from the seed, takes the rest of the window, so it begins within the first 512 tokens and ends within the last 512.
All inputs are finite; a program needn't handle non-finite values.
Results may differ from the reference program's by a relative error of at most 0.025.
Values may be sent and summed in bfloat16 or wider, within the bound.
No kernel may reach another device: no remote copies, remote signals or barrier semaphores. Data moves between devices by JAX's collectives and lax.ppermute only.
A program may use at most 192 MiB of HBM per device.

```python
import jax
import jax.numpy as jnp
from jax import lax

D = 2048
HEADS = 16
HEAD_DIM = 128
FF = 8192
ROWS = 512
DOCS = 8
WINDOW = 4096


def draw_lengths(key, part):
    key = jax.random.fold_in(key, 7)
    pair_key, order_key, place_key = jax.random.split(key, 3)
    short_most = max(1, ROWS // DOCS)
    short_count = DOCS - 1
    pair_count = short_count // 2
    firsts = jax.random.randint(pair_key, (pair_count,), 1, short_most + 1, dtype=jnp.int32)
    firsts = jnp.where(jnp.arange(pair_count, dtype=jnp.int32) == 0, 1, firsts).astype(jnp.int32)
    seconds = (short_most + 1 - firsts).astype(jnp.int32)
    middle_one = jnp.full((short_count % 2,), (short_most + 1) // 2, jnp.int32)
    shorts = jnp.concatenate([firsts, seconds, middle_one]).astype(jnp.int32)
    shorts = jax.random.permutation(order_key, shorts)
    before = jax.random.randint(place_key, (), 0, DOCS, dtype=jnp.int32)
    longest = WINDOW - jnp.sum(shorts)
    slots = jnp.arange(DOCS, dtype=jnp.int32)
    padded = jnp.concatenate([shorts, jnp.zeros((1,), jnp.int32)])
    shifted = jnp.concatenate([jnp.zeros((1,), jnp.int32), shorts])
    return jnp.where(slots < before, padded, jnp.where(slots == before, longest, shifted)).astype(jnp.int32)


def block_levels(stream_key, dims, pieces, least, high):
    def one(position, blocks):
        steps = jax.random.uniform(jax.random.fold_in(jax.random.fold_in(stream_key, 6), position), (blocks,), jnp.float32, least / len(pieces), high / len(pieces))
        return jnp.repeat(jnp.exp(steps), dims[position] // blocks).reshape((-1,) + (1,) * (len(dims) - position - 1))

    level = one(*pieces[0])
    for cut in pieces[1:]:
        level = level * one(*cut)
    return level


def scatter_about(own_key, shape, deviation, reach, pieces=(), kind=jnp.bfloat16):
    level = block_levels(own_key, shape, pieces, -0.22, 0.18) if pieces else 1.0
    values = jax.random.normal(own_key, shape, jnp.float32) * deviation * level
    return jnp.minimum(jnp.maximum(values, -reach), reach).astype(kind)


def setup_inputs(seed: int = 0) -> dict:
    keys = jax.random.split(jax.random.key(seed), 18)
    return {
        "hidden_in": scatter_about(keys[0], (WINDOW, D), 1.0, 6.0, ((0, 32),)),
        "lengths": draw_lengths(jax.random.fold_in(keys[17], 71), 0),
        "ln1_gain": jnp.clip(1.0 + 0.15 * jax.random.normal(keys[2], (D,), jnp.float32), 0.25, 1.75),
        "ln1_bias": scatter_about(keys[3], (D,), 0.5, 3.0, (), jnp.float32),
        "w_query": scatter_about(keys[4], (D, HEADS * HEAD_DIM), D ** -0.5, 0.125, ((1, 4),)),
        "b_query": scatter_about(keys[5], (HEADS * HEAD_DIM,), 0.5, 3.0, ((0, 4),), jnp.float32),
        "w_kv": scatter_about(keys[6], (D, 2 * HEAD_DIM), D ** -0.5, 0.125),
        "b_value": scatter_about(keys[7], (HEAD_DIM,), 0.02, 0.12, (), jnp.float32),
        "w_out": scatter_about(keys[8], (HEADS * HEAD_DIM, D), (max(1, HEADS * HEAD_DIM // ROWS)) ** -0.5, 3.0, ((0, 4),)),
        "b_out": scatter_about(keys[9], (D,), 0.5, 3.0, (), jnp.float32),
        "ln2_gain": jnp.clip(1.0 + 0.15 * jax.random.normal(keys[10], (D,), jnp.float32), 0.25, 1.75),
        "ln2_bias": scatter_about(keys[11], (D,), 0.5, 3.0, (), jnp.float32),
        "w_fc": scatter_about(keys[12], (D, FF), D ** -0.5, 0.125, ((1, 4),)),
        "b_fc": scatter_about(keys[13], (FF,), 0.5, 3.0, ((0, 4),), jnp.float32),
        "w_proj": scatter_about(keys[14], (FF, D), FF ** -0.5, 0.0625, ((0, 4),)),
        "b_proj": scatter_about(keys[15], (D,), 0.5, 3.0, (), jnp.float32),
        "grad_out": scatter_about(keys[16], (WINDOW, D), 1.0, 6.0, ((0, 32),)),
    }


@jax.custom_vjp
def low(v):
    return lax.optimization_barrier(v.astype(jnp.bfloat16)).astype(jnp.float32)

@jax.custom_vjp
def low_back(v):
    return v

def low_keep(v):
    return (low(v), None)

def low_pass(kept, grad):
    return (grad,)

def back_keep(v):
    return (v, None)

def back_low(kept, grad):
    return (low(grad),)
low.defvjp(low_keep, low_pass)
low_back.defvjp(back_keep, back_low)
EPS = 1e-05
NEG = -1e+30

def matmul(left, right):
    return jnp.dot(left, right, precision=lax.Precision.HIGHEST)

def layer_norm(features, gain, shift):
    centered = features - lax.optimization_barrier(jnp.mean(features, axis=-1, keepdims=True))
    variance = lax.optimization_barrier(jnp.mean(centered * centered, axis=-1, keepdims=True))
    return centered * lax.rsqrt(variance + EPS) * gain + shift

def segment_ids(lengths, length_all):
    doc_ends = jnp.cumsum(lengths)
    places = jnp.arange(length_all, dtype=jnp.int32)
    return lax.optimization_barrier(jnp.sum((doc_ends[None, :] <= places[:, None]).astype(jnp.int32), axis=1))

def attention(queries, key_rows, value_rows, segments):
    total = queries.shape[0]
    width = min(512, total)
    scaling = HEAD_DIM ** (-0.5)
    places = jnp.arange(total, dtype=jnp.int32)
    grouped = queries.reshape(total // width, width, HEADS, HEAD_DIM)
    offsets = jnp.arange(total // width, dtype=jnp.int32) * width

    def one_block(pair):
        query_block, offset = pair
        raw_scores = low_back(jnp.einsum('qhd,kd->qhk', query_block, key_rows, precision=lax.Precision.HIGHEST))
        query_place = offset + jnp.arange(width, dtype=jnp.int32)
        query_seg = lax.dynamic_slice_in_dim(segments, offset, width)
        allowed = (places[None, :] <= query_place[:, None]) & (segments[None, :] == query_seg[:, None])
        scores = jnp.where(allowed[:, None, :], raw_scores * scaling, NEG)
        weights = low(jax.nn.softmax(scores, axis=-1))
        return jnp.einsum('qhk,kd->qhd', weights, value_rows, precision=lax.Precision.HIGHEST)
    result = lax.map(jax.checkpoint(one_block), (grouped, offsets))
    return result.reshape(total, HEADS * HEAD_DIM)

def forward(hidden, ln1_gain, ln1_bias, w_query, b_query, w_kv, b_value, w_out, b_out, ln2_gain, ln2_bias, w_fc, b_fc, w_proj, b_proj, segments):
    normed_one = low(layer_norm(hidden, ln1_gain, ln1_bias))
    queries = low(low_back(matmul(normed_one, w_query)) + b_query)
    bias_row = jnp.concatenate([jnp.zeros_like(b_value), b_value])
    key_value = low(low_back(matmul(normed_one, w_kv)) + bias_row)
    attended = low(low_back(attention(queries, key_value[:, :HEAD_DIM], key_value[:, HEAD_DIM:], segments)))
    middle = hidden + low_back(matmul(attended, w_out)) + b_out
    normed_two = low(layer_norm(middle, ln2_gain, ln2_bias))
    pre_act = low_back(matmul(normed_two, w_fc)) + b_fc
    activated = low(jax.nn.gelu(pre_act, approximate=True))
    return middle + low_back(matmul(activated, w_proj)) + b_proj

def reference(hidden_in, lengths, ln1_gain, ln1_bias, w_query, b_query, w_kv, b_value, w_out, b_out, ln2_gain, ln2_bias, w_fc, b_fc, w_proj, b_proj, grad_out):
    segments = segment_ids(lengths, WINDOW)
    primals = (hidden_in.astype(jnp.float32), ln1_gain, ln1_bias, w_query.astype(jnp.float32), b_query, w_kv.astype(jnp.float32), b_value, w_out.astype(jnp.float32), b_out, ln2_gain, ln2_bias, w_fc.astype(jnp.float32), b_fc, w_proj.astype(jnp.float32), b_proj)
    result, backward = jax.vjp(lambda *params: forward(*params, segments), *primals)
    grads = backward(grad_out.astype(jnp.float32))
    return (result.astype(jnp.bfloat16), grads[0], grads[1], grads[2], grads[3], grads[4], grads[5], grads[6], grads[7], grads[8], grads[9], grads[10], grads[11], grads[12], grads[13], grads[14])
```

```python
import functools
import math

import jax
import jax.numpy as jnp
from jax import lax
from jax.experimental import pallas as pl
from jax.experimental.pallas import tpu as pltpu
from jax.sharding import PartitionSpec as P

EPS = 1e-05
NEG = -1e30
LOG2E = math.log2(math.e)
VMEM_LIMIT = 60 * 1024 * 1024
LIGHT = pl.CostEstimate(flops=1024, bytes_accessed=1024, transcendentals=0)
NT = (((1,), (1,)), ((), ()))


def dot(left, right):
    return jnp.dot(left, right, preferred_element_type=jnp.float32)


def dot_nt(left, right):
    return lax.dot_general(left, right, NT, preferred_element_type=jnp.float32)


def tie(value, *deps):
    return lax.optimization_barrier((value, *deps))[0]


def struct(shape, dtype):
    return jax.ShapeDtypeStruct(shape, dtype)


def swap(value, axis, bit):
    count = lax.axis_size(axis)
    return lax.ppermute(value, axis, [(j, j ^ bit) for j in range(count)])


def gather_rows(own):
    beside = swap(own, "tp", 1)
    across = swap(own, "tp", 2)
    return own, beside, across, swap(across, "tp", 1)


def gather_other(own, first, second):
    across = swap(tie(own, first), "tp", 2)
    return own, swap(tie(own, first), "tp", 1), across, swap(tie(across, second), "tp", 1)


def call(kernel, outs, *args):
    return pl.pallas_call(
        kernel,
        out_shape=outs,
        compiler_params=pltpu.CompilerParams(vmem_limit_bytes=VMEM_LIMIT),
        cost_estimate=LIGHT,
    )(*args)


def total(*refs):
    return sum(ref[...].astype(jnp.float32) for ref in refs)


def add_kernel(*refs):
    refs[-1][...] = total(*refs[:-1]).astype(jnp.bfloat16)


def add_low(*values):
    return call(add_kernel, struct(values[0].shape, jnp.bfloat16), *values)


def split_kernel(meta, keep_in, got_in, send_ref, keep_ref):
    both = total(keep_in, got_in).astype(jnp.bfloat16)

    @pl.when(pl.program_id(1) == 0)
    def _():
        send_ref[...] = both

    @pl.when(pl.program_id(1) == 1)
    def _():
        keep_ref[...] = both


def halves_kernel(side, keep, got, mine, theirs):
    half = mine.shape[1]
    both = total(keep, got).astype(jnp.bfloat16)
    low, high = both[:, :half], both[:, half:]
    mine[...] = jnp.where(side[0] == 0, low, high)
    theirs[...] = jnp.where(side[0] == 0, high, low)


def split_add(side, keep, got):
    parts, rows, columns = keep.shape
    block = pl.BlockSpec((1, rows, columns), lambda m, s, meta: (2 * m + (meta[0] + 1 - s) % 2, 0, 0))
    half = struct((parts // 2, rows, columns), jnp.bfloat16)
    return pl.pallas_call(
        split_kernel,
        grid_spec=pltpu.PrefetchScalarGridSpec(
            num_scalar_prefetch=1,
            grid=(parts // 2, 2),
            in_specs=[block, block],
            out_specs=[pl.BlockSpec((1, rows, columns), lambda m, s, meta: (m, 0, 0))] * 2,
        ),
        out_shape=[half, half],
        compiler_params=pltpu.CompilerParams(vmem_limit_bytes=VMEM_LIMIT),
        cost_estimate=LIGHT,
    )(jnp.stack([side]).astype(jnp.int32), keep, got)


def line_bits():
    bit = 2
    while bit < lax.axis_size("seq"):
        yield bit
        bit *= 2


def column_halves(value):
    side = lax.axis_index("seq") % 2
    half = value.shape[1] // 2
    keep = lax.dynamic_slice_in_dim(value, side * half, half, 1)
    send = lax.dynamic_slice_in_dim(value, (1 - side) * half, half, 1)
    return keep, send


def sum_over(value, axis):
    bit = 1
    while bit < lax.axis_size(axis):
        value = value + swap(value, axis, bit)
        bit *= 2
    return value


def normalized(features):
    centered = features - jnp.mean(features, axis=-1, keepdims=True)
    variance = jnp.mean(centered * centered, axis=-1, keepdims=True)
    scale = lax.rsqrt(variance + EPS)
    return centered * scale, scale


def norm_back(features, gain, grads):
    normed, scale = normalized(features)
    scaled = grads * gain
    mean = jnp.mean(scaled, axis=-1, keepdims=True)
    along = jnp.mean(scaled * normed, axis=-1, keepdims=True)
    over_rows = lambda value: jnp.sum(value, axis=0, keepdims=True)
    return scale * (scaled - mean - normed * along), over_rows(grads * normed), over_rows(grads)


def first_kernel(in_ref, gain, shift, w_ref, bias, norm_ref, key_ref, value_ref):
    normed, _ = normalized(in_ref[...].astype(jnp.float32))
    low = (normed * gain[...] + shift[...]).astype(jnp.bfloat16)
    norm_ref[...] = low
    pairs = dot(low, w_ref[...])
    hd = key_ref.shape[1]
    key_ref[...] = pairs[:, :hd].astype(jnp.bfloat16)
    value_ref[...] = (pairs[:, hd:] + bias[...]).astype(jnp.bfloat16)


def query_kernel(r0, r1, r2, r3, w_ref, bias, out_ref):
    rows = jnp.concatenate([r0[...], r1[...], r2[...], r3[...]], axis=0)
    out_ref[...] = (dot(rows, w_ref[...]) + bias[...]).astype(jnp.bfloat16)


def project_kernel(first, form, value_ref, w_ref, out0, out1):
    size = out0.shape[0]
    result = form(value_ref[first * size : (first + 2) * size, :], w_ref[...]).astype(jnp.bfloat16)
    out0[...] = result[:size]
    out1[...] = result[size:]


def middle_kernel(in_ref, p0, p1, p2, bias, gain, shift, middle_ref, norm_ref):
    middle = total(in_ref, p0, p1, p2) + bias[...]
    middle_ref[...] = middle
    normed, _ = normalized(middle)
    norm_ref[...] = (normed * gain[...] + shift[...]).astype(jnp.bfloat16)


def middle_back_kernel(middle_ref, p0, p1, p2, up_ref, gain, grads_ref, low_ref, sums_ref):
    upstream = up_ref[...].astype(jnp.float32)
    back, for_gain, for_shift = norm_back(middle_ref[...], gain[...], total(p0, p1, p2))
    grads = upstream + back
    grads_ref[...] = grads
    low_ref[...] = grads.astype(jnp.bfloat16)
    sums_ref[0:1] = jnp.sum(upstream, axis=0, keepdims=True)
    sums_ref[1:2] = for_gain
    sums_ref[2:3] = for_shift
    sums_ref[3:4] = jnp.sum(grads, axis=0, keepdims=True)


def attended_grads_kernel(r0, r1, r2, r3, w_ref, out_ref):
    rows = jnp.concatenate([r0[...], r1[...], r2[...], r3[...]], axis=0)
    out_ref[...] = dot_nt(rows, w_ref[...]).astype(jnp.bfloat16)


def layer_kernel(middle_ref, p0, p1, p2, bias, out_ref):
    out_ref[...] = (total(middle_ref, p0, p1, p2) + bias[...]).astype(jnp.bfloat16)


def last_kernel(in_ref, p0, p1, p2, pairs_ref, w_ref, middle_ref, gain, grads_ref, sums_ref, value_ref):
    hd = value_ref.shape[1]
    grads = total(p0, p1, p2) + dot_nt(pairs_ref[...], w_ref[...])
    back, for_gain, for_shift = norm_back(in_ref[...].astype(jnp.float32), gain[...], grads)
    grads_ref[...] = middle_ref[...] + back
    sums_ref[0:1] = for_gain
    sums_ref[1:2] = for_shift
    value_ref[...] = jnp.sum(pairs_ref[:, hd:].astype(jnp.float32), axis=0, keepdims=True)


def turned(own_ref, other_ref, scratch):
    half = own_ref.shape[0]
    scratch[:, :half] = own_ref[...].T
    scratch[:, half:] = other_ref[...].T


def weight_kernel(meta, *refs):
    lefts, own_ref, other_ref = refs[:8], refs[8], refs[9]
    send_ref, keep_ref, scratch = refs[10:]

    @pl.when((pl.program_id(0) == 0) & (pl.program_id(1) == 0))
    def _():
        turned(own_ref, other_ref, scratch)

    rows = jnp.concatenate([ref[...] for ref in lefts], axis=0)
    part = dot(scratch[...], rows).astype(jnp.bfloat16)

    @pl.when(pl.program_id(1) == 0)
    def _():
        send_ref[0] = part

    @pl.when(pl.program_id(1) == 1)
    def _():
        keep_ref[0] = part


def weight_grads(blocks, lowest, own, piece, other):
    count, columns = other.shape
    size, dim = blocks[0].shape
    parts = lax.axis_size("seq") // 2
    tile = dim // parts
    block = pl.BlockSpec((size, tile), lambda m, s, meta: (0, 2 * m + (meta[0] + 1 - s) % 2))
    half = struct((parts // 2, columns, tile), jnp.bfloat16)
    return pl.pallas_call(
        weight_kernel,
        grid_spec=pltpu.PrefetchScalarGridSpec(
            num_scalar_prefetch=1,
            grid=(parts // 2, 2),
            in_specs=[block] * 8
            + [
                pl.BlockSpec((count, columns), lambda m, s, meta: (0, piece)),
                pl.BlockSpec((count, columns), lambda m, s, meta: (0, 0)),
            ],
            out_specs=[pl.BlockSpec((1, columns, tile), lambda m, s, meta: (m, 0, 0))] * 2,
            scratch_shapes=[pltpu.VMEM((columns, 2 * count), jnp.bfloat16)],
        ),
        out_shape=[half, half],
        compiler_params=pltpu.CompilerParams(vmem_limit_bytes=VMEM_LIMIT),
        cost_estimate=LIGHT,
    )(lowest, *blocks, own, other)


def slab_kernel(meta, *refs):
    lefts, own_ref, other_ref, out_ref, scratch = refs[:8], *refs[8:]
    turned(own_ref, other_ref, scratch)
    rows = jnp.concatenate([ref[...] for ref in lefts], axis=0)
    out_ref[...] = dot(scratch[...], rows).astype(jnp.bfloat16)


def slab_grads(blocks, slab, own, other, parts):
    count, columns = own.shape
    size, dim = blocks[0].shape
    tile = dim // parts
    block = pl.BlockSpec((size, tile), lambda m, meta: (0, meta[0]))
    fixed = pl.BlockSpec((count, columns), lambda m, meta: (0, 0))
    return pl.pallas_call(
        slab_kernel,
        grid_spec=pltpu.PrefetchScalarGridSpec(
            num_scalar_prefetch=1,
            grid=(1,),
            in_specs=[block] * 8 + [fixed, fixed],
            out_specs=pl.BlockSpec((columns, tile), lambda m, meta: (0, 0)),
            scratch_shapes=[pltpu.VMEM((columns, 2 * count), jnp.bfloat16)],
        ),
        out_shape=struct((columns, tile), jnp.bfloat16),
        compiler_params=pltpu.CompilerParams(vmem_limit_bytes=VMEM_LIMIT),
        cost_estimate=LIGHT,
    )(slab, *blocks, own, other)


ANYWHERE = pl.BlockSpec(memory_space=pl.ANY)


def mlp_kernel(tiles, aliased, meta, x0, x1, g0, g1, fc_ref, proj_ref, bias_ref, *refs):
    (a0, a1, ak, l0, l1, lk, m0, m1, t0, t1, sum_ref, x_ref, g_ref, macc, tacc) = refs[aliased:]
    step = pl.program_id(0)
    size = x0.shape[0]

    @pl.when(step == 0)
    def _():
        x_ref[:size] = x0[...]
        x_ref[size:] = x1[...]
        g_ref[:size] = g0[...]
        g_ref[size:] = g1[...]

    values = dot(x_ref[...], fc_ref[...]) + bias_ref[...]
    grads = dot_nt(g_ref[...], proj_ref[...])
    root = math.sqrt(2 / math.pi)
    square = values * values
    bend = jnp.tanh(root * values * (1 + 0.044715 * square))
    half = 0.5 * (1 + bend)
    slope = half + 0.5 * root * values * (1 - bend * bend) * (1 + 3 * 0.044715 * square)
    activated = (values * half).astype(jnp.bfloat16)
    grads = grads * slope
    sum_ref[...] = jnp.sum(grads, axis=0, keepdims=True)
    low = grads.astype(jnp.bfloat16)

    @pl.when(step == 0)
    def _():
        macc[...] = jnp.zeros_like(macc)
        tacc[...] = jnp.zeros_like(tacc)

    chunk = macc.shape[1] // 4
    for c in range(4):
        cut = slice(c * chunk, (c + 1) * chunk)
        macc[:, cut] += dot(activated, proj_ref[:, cut])
        tacc[:, cut] += dot_nt(low, fc_ref[cut, :])

    @pl.when(step < tiles // 4)
    def _():
        a0[...] = activated
        l0[...] = low

    @pl.when((step >= tiles // 4) & (step < tiles // 2))
    def _():
        a1[...] = activated
        l1[...] = low

    @pl.when(step >= tiles // 2)
    def _():
        ak[...] = activated
        lk[...] = low

    @pl.when(step == tiles - 1)
    def _():
        f = macc[...].astype(jnp.bfloat16)
        b = tacc[...].astype(jnp.bfloat16)
        m0[...] = f[:size]
        m1[...] = f[size:]
        t0[...] = b[:size]
        t1[...] = b[size:]


def mlp(blocks, ups, side, first, w_fc, w_proj, b_fc, before=()):
    size, dim = blocks[0].shape
    hidden = w_fc.shape[1]
    tiles = 4
    width = hidden // tiles
    tile = lambda n, meta: ((n // (tiles // 2)) ^ (1 - meta[0])) * (tiles // 2) + n % (tiles // 2)
    within = lambda n, start, count: jnp.clip(n - start, 0, count - 1)
    fixed = pl.BlockSpec((size, dim), lambda n, meta: (0, 0))
    columns = lambda start, count: pl.BlockSpec(
        (2 * size, width), lambda n, meta: (first // 2, within(n, start, count))
    )
    spread = [columns(0, tiles // 4), columns(tiles // 4, tiles // 4), columns(tiles // 2, tiles // 2)] * 2
    shapes = [struct((4 * size, hidden // 4), jnp.bfloat16)] * 2 + [struct((4 * size, hidden // 2), jnp.bfloat16)]
    rows = struct((size, dim), jnp.bfloat16)
    return pl.pallas_call(
        functools.partial(mlp_kernel, tiles, len(before)),
        grid_spec=pltpu.PrefetchScalarGridSpec(
            num_scalar_prefetch=1,
            grid=(tiles,),
            in_specs=[fixed] * 4
            + [
                pl.BlockSpec((dim, width), lambda n, meta: (0, tile(n, meta))),
                pl.BlockSpec((width, dim), lambda n, meta: (tile(n, meta), 0)),
                pl.BlockSpec((1, width), lambda n, meta: (0, tile(n, meta))),
            ]
            + [ANYWHERE] * len(before),
            out_specs=spread + [fixed] * 4 + [pl.BlockSpec((1, width), lambda n, meta: (0, tile(n, meta)))],
            scratch_shapes=[pltpu.VMEM((2 * size, dim), jnp.bfloat16)] * 2 + [pltpu.VMEM((2 * size, dim), jnp.float32)] * 2,
        ),
        out_shape=shapes * 2 + [rows] * 4 + [struct((1, hidden), jnp.float32)],
        input_output_aliases={8 + j: j for j in range(len(before))},
        compiler_params=pltpu.CompilerParams(vmem_limit_bytes=VMEM_LIMIT),
        cost_estimate=LIGHT,
    )(side, *blocks, *ups, w_fc, w_proj, b_fc[None, :], *before)


def allowed_pairs(slot, masks_ref, rows_ref, keys_ref):
    place = keys_ref[...] + masks_ref[2, slot]
    return (place <= rows_ref[0:1, :]) & (place >= rows_ref[1:2, :])


def when_live(meta, slot, visit):
    @pl.when((meta[0, slot] == 1) & (meta[1, slot] == 0))
    def _():
        visit(True)

    @pl.when((meta[0, slot] == 1) & (meta[1, slot] == 1))
    def _():
        visit(False)


def forward_kernel(heads, meta, q_ref, *refs):
    key_refs, value_refs = refs[:4], refs[4:8]
    rows_ref, keys_ref, out_ref, norm_ref, m_ref, l_ref, acc_ref = refs[8:]
    hd = q_ref.shape[1] // heads
    scale = hd ** (-0.5) * LOG2E
    slots = key_refs[0].shape[0]

    def visit(slot, masked, exact):
        keys = jnp.concatenate([ref[slot] for ref in key_refs], axis=0)
        values_t = jnp.concatenate([ref[slot] for ref in value_refs], axis=0).T
        if masked:
            allowed = allowed_pairs(slot, meta, rows_ref, keys_ref)
        for h in range(heads):
            scores = dot_nt(keys, q_ref[:, h * hd : (h + 1) * hd]) * scale
            if masked:
                scores = jnp.where(allowed, scores, NEG)
            top = m_ref[h : h + 1, :]
            if exact:
                new = jnp.maximum(top, jnp.max(scores, axis=0, keepdims=True))
                decay = jnp.exp2(top - new)
                m_ref[h : h + 1, :] = new
                l_ref[h : h + 1, :] = l_ref[h : h + 1, :] * decay
                acc_ref[h] = acc_ref[h] * decay
                top = new
            weights = jnp.exp2(scores - top)
            l_ref[h : h + 1, :] += jnp.sum(weights, axis=0, keepdims=True)
            acc_ref[h] += dot(values_t, weights.astype(jnp.bfloat16))

    def run(exact):
        m_ref[...] = jnp.full_like(m_ref, NEG)
        l_ref[...] = jnp.zeros_like(l_ref)
        acc_ref[...] = jnp.zeros_like(acc_ref)
        visit(0, True, True)

        def body(slot, carry):
            when_live(meta, slot, lambda masked: visit(slot, masked, exact))
            return carry

        lax.fori_loop(1, slots, body, 0)

    run(False)

    @pl.when(jnp.logical_not(jnp.max(l_ref[...]) < 2.0**100))
    def _():
        run(True)

    norm_ref[...] = m_ref[...] + jnp.log2(l_ref[...])
    for h in range(heads):
        result = acc_ref[h] / l_ref[h : h + 1, :]
        out_ref[:, h * hd : (h + 1) * hd] = result.T.astype(jnp.bfloat16)


def backward_visit(heads, slot, meta, q_ref, key_refs, value_refs, rows_ref, keys_ref, norm_ref, up_ref, delta_ref, dq_acc, d_refs):
    hd = q_ref.shape[1] // heads
    part = key_refs[0].shape[1]
    scale = hd ** (-0.5)

    def visit(masked):
        keys = jnp.concatenate([ref[0] for ref in key_refs], axis=0)
        values = jnp.concatenate([ref[0] for ref in value_refs], axis=0)
        keys_t = keys.T
        if masked:
            allowed = allowed_pairs(slot, meta, rows_ref, keys_ref)
        dk = dv = None
        for h in range(heads):
            q = q_ref[:, h * hd : (h + 1) * hd]
            up = up_ref[:, h * hd : (h + 1) * hd]
            weights = jnp.exp2(dot_nt(keys, q) * (scale * LOG2E) - norm_ref[h : h + 1, :])
            if masked:
                weights = jnp.where(allowed, weights, 0.0)
            grads = dot_nt(values, up)
            score_grads = (weights * (grads - delta_ref[h : h + 1, :])).astype(jnp.bfloat16)
            dv_h = dot(weights.astype(jnp.bfloat16), up)
            dk_h = dot(score_grads, q)
            dv = dv_h if dv is None else dv + dv_h
            dk = dk_h if dk is None else dk + dk_h
            dq_acc[h] = dq_acc[h] + dot(keys_t, score_grads)
        for index, ref in enumerate(d_refs):
            part_rows = slice(index * part, (index + 1) * part)
            ref[0, :, :hd] = (dk[part_rows] * scale).astype(jnp.bfloat16)
            ref[0, :, hd:] = dv[part_rows].astype(jnp.bfloat16)

    @pl.when(meta[0, slot] == 0)
    def _():
        for ref in d_refs:
            ref[...] = jnp.zeros_like(ref)

    when_live(meta, slot, visit)


def backward_first_kernel(heads, first, meta, q_ref, *refs):
    key_refs, value_refs = refs[:4], refs[4:8]
    rows_ref, keys_ref, norm_ref, up_ref, att_ref, acc_ref, delta_ref = refs[8:15]
    d_refs = refs[15:19]
    hd = q_ref.shape[1] // heads

    @pl.when(pl.program_id(0) == 0)
    def _():
        acc_ref[...] = jnp.zeros_like(acc_ref)
        for h in range(heads):
            cols = slice(h * hd, (h + 1) * hd)
            both = att_ref[:, cols].astype(jnp.float32) * up_ref[:, cols].astype(jnp.float32)
            delta_ref[h : h + 1, :] = jnp.sum(both.T, axis=0, keepdims=True)

    slot = pl.program_id(0) + first
    backward_visit(heads, slot, meta, q_ref, key_refs, value_refs, rows_ref, keys_ref, norm_ref, up_ref, delta_ref, acc_ref, d_refs)


def backward_last_kernel(heads, first, meta, q_ref, *refs):
    key_refs, value_refs = refs[:4], refs[4:8]
    rows_ref, keys_ref, norm_ref, up_ref, start_ref, delta_ref, dq_ref, bias_ref = refs[8:16]
    d_refs = refs[16:20]
    acc_ref = refs[20]
    hd = q_ref.shape[1] // heads

    @pl.when(pl.program_id(0) == 0)
    def _():
        acc_ref[...] = start_ref[...]

    slot = pl.program_id(0) + first
    backward_visit(heads, slot, meta, q_ref, key_refs, value_refs, rows_ref, keys_ref, norm_ref, up_ref, delta_ref, acc_ref, d_refs)

    @pl.when(pl.program_id(0) == pl.num_programs(0) - 1)
    def _():
        for h in range(heads):
            result = (acc_ref[h] * hd ** (-0.5)).T
            bias_ref[:, h * hd : (h + 1) * hd] = jnp.sum(result, axis=0, keepdims=True)
            dq_ref[:, h * hd : (h + 1) * hd] = result.astype(jnp.bfloat16)


def whole(value):
    return pl.BlockSpec(value.shape, lambda step, meta: (0,) * len(value.shape))


def attention_call(kernel, meta, first, steps, slots, queries, keys, values, extra, outs, scratch, passes):
    rows, width = queries.shape
    part, hd = keys[0].shape[1:]
    block = lambda columns, start: pl.BlockSpec((slots // steps, part, columns), lambda step, meta: (step + start, 0, 0))
    heads = width // hd
    return pl.pallas_call(
        kernel,
        grid_spec=pltpu.PrefetchScalarGridSpec(
            num_scalar_prefetch=1,
            grid=(steps,),
            in_specs=[whole(queries)] + [block(hd, first)] * 8 + [whole(value) for value in extra],
            out_specs=[block(2 * hd, 0) if out.shape == (slots, part, 2 * hd) else whole(out) for out in outs],
            scratch_shapes=scratch,
        ),
        out_shape=outs,
        compiler_params=pltpu.CompilerParams(vmem_limit_bytes=VMEM_LIMIT),
        cost_estimate=LIGHT,
    )(meta, queries, *keys, *values, *extra)


def attention_forward(queries, keys, values, meta, rows_info, keys_info, heads):
    rows, width = queries.shape
    return attention_call(
        functools.partial(forward_kernel, heads), meta, 0, 1, keys[0].shape[0], queries, keys, values,
        [rows_info, keys_info],
        [struct((rows, width), jnp.bfloat16), struct((heads, rows), jnp.float32)],
        [
            pltpu.VMEM((heads, rows), jnp.float32),
            pltpu.VMEM((heads, rows), jnp.float32),
            pltpu.VMEM((heads, width // heads, rows), jnp.float32),
        ],
        2,
    )


def backward_calls(queries, keys, values, meta, rows_info, keys_info, norm, attended, upstream, heads):
    rows, width = queries.shape
    hd = width // heads
    n, part = keys[0].shape[:2]
    half = n // 2
    grads = [struct((half, part, 2 * hd), jnp.bfloat16)] * 4
    shared = [rows_info, keys_info, norm, upstream]

    def first(*deps):
        return attention_call(
            functools.partial(backward_first_kernel, heads, half), meta, half, half, half, tie(queries, *deps),
            keys, values, shared + [attended],
            [struct((heads, hd, rows), jnp.float32), struct((heads, rows), jnp.float32)] + grads,
            [], 5,
        )

    def last(start, delta, *deps):
        return attention_call(
            functools.partial(backward_last_kernel, heads, 0), meta, 0, half, half, tie(queries, *deps),
            keys, values, shared + [start, delta],
            [struct((rows, width), jnp.bfloat16), struct((1, width), jnp.float32)] + grads,
            [pltpu.VMEM((heads, hd, rows), jnp.float32)], 5,
        )

    return first, last


def gather_slots(own, bits, axis):
    found = {0: own}
    for bit in bits:
        masks = sorted(found)
        stacked = jnp.stack([found[m] for m in masks])
        got = swap(stacked, axis, bit)
        found.update({m ^ bit: got[j] for j, m in enumerate(masks)})
    return found


def body(
    hidden_in, lengths, ln1_gain, ln1_bias, w_query, b_query, w_kv, b_value, w_out, b_out,
    ln2_gain, ln2_bias, w_fc, b_fc, w_proj, b_proj, grad_out,
):
    seq_count = lax.axis_size("seq")
    tp_count = lax.axis_size("tp")
    seq_index = lax.axis_index("seq")
    tp_index = lax.axis_index("tp")
    own_rows, dim = hidden_in.shape
    group_rows = own_rows * tp_count
    head_dim = b_value.shape[0]
    heads = w_query.shape[1] // head_dim
    joined = lambda *blocks: jnp.concatenate(blocks, axis=0)
    seq_bits = [1 << j for j in range(seq_count.bit_length() - 1)]

    order = jnp.stack([tp_index, tp_index ^ 1, tp_index ^ 2, tp_index ^ 3]).astype(jnp.int32)
    inside = (order[:, None] * own_rows + jnp.arange(own_rows, dtype=jnp.int32)[None, :]).reshape(-1)
    group_first = seq_index * group_rows
    doc_ends = jnp.cumsum(lengths)
    begins = jnp.max(
        jnp.where(doc_ends[None, :] <= (inside + group_first)[:, None], doc_ends[None, :], 0), axis=1
    )
    rows_info = jnp.stack([inside, begins - group_first])
    keys_info = inside[:, None]
    slot_group = seq_index ^ jnp.arange(seq_count, dtype=jnp.int32)
    key_first = slot_group * group_rows
    live = (slot_group <= seq_index) & (key_first + group_rows > jnp.min(begins))
    clear = (slot_group < seq_index) & (key_first >= jnp.max(begins))
    meta = jnp.stack([live, clear, key_first - group_first]).astype(jnp.int32)
    side = seq_index % 2
    scalar = lambda value: jnp.stack([value]).astype(jnp.int32)
    lowest, slab, side_scalar = scalar((seq_index // 2) % 2), scalar(2 * tp_index + side), scalar(side)
    beside = lambda value: swap(value, "seq", 1)

    row = lambda vector: vector[None, :]
    rows_low = struct((own_rows, dim), jnp.bfloat16)
    rows_wide = struct((own_rows, dim), jnp.float32)
    narrow = struct((own_rows, head_dim), jnp.bfloat16)
    normed_one, key_own, value_own = call(
        first_kernel, [rows_low, narrow, narrow], hidden_in, row(ln1_gain), row(ln1_bias), w_kv, row(b_value)
    )
    key_slots = gather_slots(key_own, seq_bits[::-1], "seq")
    key_stack = jnp.stack([key_slots[m] for m in range(seq_count)])
    value_two = jnp.stack([value_own, swap(value_own, "tp", 2)])
    value_slots = gather_slots(value_two, seq_bits[::-1], "seq")
    value_two = jnp.stack([value_slots[m] for m in range(seq_count)], axis=1)
    value_beside = swap(value_two, "tp", 1)
    values = [value_two[0], value_beside[0], value_two[1], value_beside[1]]
    blocks_one = gather_rows(normed_one)
    queries = call(
        query_kernel, struct((group_rows, heads * head_dim), jnp.bfloat16), *blocks_one, w_query, row(b_query)
    )
    key_across = tie(swap(key_stack, "tp", 2), queries)
    keys = [key_stack, swap(key_stack, "tp", 1), key_across, swap(key_across, "tp", 1)]
    up_other, one_other = beside(grad_out), beside(normed_one)
    ups_own = gather_rows(tie(grad_out, queries))
    attended, norm = attention_forward(queries, keys, values, meta, rows_info, keys_info, heads)

    def project(value, weight, form):
        far = call(functools.partial(project_kernel, 2, form), [rows_low] * 2, value, weight)
        near = call(functools.partial(project_kernel, 0, form), [rows_low] * 2, tie(value, far[0]), weight)
        return (*near, *far)

    def scatter(own, beside, across, opposite, *deps):
        over = add_low(tie(across, *deps), swap(opposite, "tp", 1))
        return own, swap(beside, "tp", 1), over, swap(over, "tp", 2)

    att0, att1, _, att2 = scatter(*project(attended, w_out, dot))
    middle, normed_two = call(
        middle_kernel, [rows_wide, rows_low], hidden_in, att0, att1, att2, row(b_out), row(ln2_gain), row(ln2_bias)
    )

    two_beside, two_across = swap(normed_two, "tp", 1), swap(normed_two, "tp", 2)
    two_other = beside(normed_two)
    *kept, mlp0, mlp1, two0, two1, sum_near = mlp(
        (normed_two, two_beside), ups_own[:2], side_scalar, 0, w_fc, w_proj, b_fc
    )
    two_across = tie(two_across, two0)
    two_opposite = swap(two_across, "tp", 1)
    *kept, mlp2, mlp3, two2, two3, sum_far = mlp(
        (two_across, two_opposite), ups_own[2:], side_scalar, 2, w_fc, w_proj, b_fc, kept
    )
    act_send0, act_send1, act_keep, low_send0, low_send1, low_keep = kept

    line = list(line_bits())
    line_side = lambda bit: (seq_index // bit) % 2

    def start_sum(blocks, keep, piece, other):
        send, kept = weight_grads(blocks, lowest, keep, piece, other)
        return kept, swap(send, "seq", line[0]), line[1:]

    def step_sum(state, *deps):
        keep, got, bits = state
        if not bits:
            return state
        keep = tie(keep, *deps)
        send, kept = split_add(line_side(bits[0]), keep, got)
        return kept, swap(send, "seq", bits[0]), bits[1:]

    def finish_sum(state, *deps):
        while state[2]:
            state = step_sum(state)
        keep, got = tie(state[0][0], *deps), state[1][0]
        half = keep.shape[1] // 2
        return pl.pallas_call(
            halves_kernel,
            in_specs=[pl.BlockSpec(memory_space=pltpu.SMEM), pl.BlockSpec(keep.shape), pl.BlockSpec(keep.shape)],
            out_shape=[struct((keep.shape[0], half), jnp.bfloat16)] * 2,
            compiler_params=pltpu.CompilerParams(vmem_limit_bytes=VMEM_LIMIT),
            cost_estimate=LIGHT,
        )(side_scalar, keep, got)

    def exchange(*halves):
        mine, theirs = joined(*[half[0] for half in halves]), beside(joined(*[half[1] for half in halves]))
        low_first = jnp.where(side == 0, mine, theirs)
        high = jnp.where(side == 0, theirs, mine)
        return joined(low_first, high).astype(jnp.float32)

    act_other0 = beside(act_send0)
    two_sum0, two_sum1, two_over, two_sum2 = scatter(two0, two1, two2, two3)
    ups = ups_own + gather_other(up_other, two0, two_over)
    sum_p0 = start_sum(ups, tie(act_keep, two_over), 0, act_other0)
    act_other1 = beside(tie(act_send1, sum_p0[0]))
    middle_grads, middle_low, sums_two = call(
        middle_back_kernel,
        [rows_wide, rows_low, struct((4, dim), jnp.float32)],
        middle, tie(two_sum0, sum_p0[0]), two_sum1, two_sum2, grad_out, row(ln2_gain),
    )
    mid_beside, mid_across = swap(middle_low, "tp", 1), swap(middle_low, "tp", 2)
    sum_p1 = start_sum(ups, tie(act_keep, middle_low), 1, act_other1)
    low_other0 = beside(tie(low_send0, sum_p1[0]))

    mid_across = tie(mid_across, sum_p1[0])
    mid_opposite = swap(mid_across, "tp", 1)
    mids_own = (middle_low, mid_beside, mid_across, mid_opposite)
    attended_grads = call(
        attended_grads_kernel, struct(attended.shape, jnp.bfloat16), *mids_own, w_out
    )
    mlp_sum0, mlp_sum1, _, mlp_sum2 = scatter(mlp0, mlp1, mlp2, mlp3, attended_grads)
    sum_p0 = step_sum(sum_p0, attended_grads)
    att_keep, att_send = column_halves(attended)

    back = backward_calls(queries, keys, values, meta, rows_info, keys_info, norm, attended, attended_grads, heads)
    start, delta, *kv_far = back[0](sum_p0[0])
    low_other1 = beside(tie(low_send1, start))
    mid_other = beside(tie(middle_low, start))
    far0, far1, far_over, far2 = scatter(*kv_far, start)
    twos = (normed_two, two_beside, two_across, two_opposite) + gather_other(two_other, attended_grads, start)
    sum_f0 = start_sum(twos, tie(low_keep, far_over), 0, low_other0)
    sum_p1 = step_sum(sum_p1, sum_f0[0])
    query_low, bias_query, *kv_near = back[1](start, delta, sum_p1[0])

    one = project(query_low, w_query, dot_nt)
    dq_keep, dq_send = column_halves(query_low)
    dq_other = beside(dq_send)
    att_other = beside(tie(att_send, query_low))
    near0, near1, near_over, near2 = scatter(*kv_near, one[0])
    one0, one1, one_over, one2 = scatter(*one, near_over)
    far_sum = add_low(tie(far0, one_over), far1, far2)
    far_there = swap(far_sum, "seq", seq_count // 2)
    sum_f1 = start_sum(twos, tie(low_keep, far_sum), 1, low_other1)
    done_p0 = finish_sum(sum_p0, sum_f1[0])
    kv_slots = add_low(tie(near0, done_p0[0]), near1, near2, far_there)
    sum_f0 = step_sum(sum_f0, kv_slots)
    ones = blocks_one + gather_other(one_other, start, kv_slots)
    sum_q = start_sum(ones, tie(dq_keep, sum_f0[0]), 0, dq_other)
    for bit in seq_bits[-2::-1]:
        kv_slots = add_low(tie(kv_slots[:bit], sum_q[0]), swap(kv_slots[bit:], "seq", bit))
    kv_low = kv_slots[0]
    kv_group = joined(*gather_rows(kv_low))
    kv_beside = beside(kv_group)
    grad_in, sums_one, sums_value = call(
        last_kernel,
        [rows_wide, struct((2, dim), jnp.float32), struct((1, head_dim), jnp.float32)],
        hidden_in, one0, one1, one2, kv_low, w_kv, middle_grads, row(ln1_gain),
    )
    mids = mids_own + gather_other(mid_other, far_sum, sums_value)
    sum_o = start_sum(mids, tie(att_keep, sums_value), 0, att_other)
    done_p1 = finish_sum(sum_p1, sum_o[0])
    sum_f1 = step_sum(sum_f1, done_p1[0])
    layer_out = call(layer_kernel, rows_low, tie(middle, sum_f1[0]), mlp_sum0, mlp_sum1, mlp_sum2, row(b_proj))

    vectors = [sums_two.reshape(-1), sums_one.reshape(-1), sums_value[0]]
    split = [bias_query[0], (sum_near + sum_far)[0]]
    vectors = jnp.concatenate(vectors + split).reshape(-1, 128)
    vectors = sum_over(vectors, "seq").reshape(-1)
    count = 6 * dim + head_dim
    shared = sum_over(vectors[:count].reshape(-1, 128), "tp").reshape(-1)
    split = vectors[count:]
    queries_width = bias_query.shape[1]

    part_kv = slab_grads(ones, slab, tie(kv_group, sum_f1[0]), kv_beside, 2 * tp_count)
    for bit in seq_bits[1:]:
        part_kv = add_low(part_kv, swap(part_kv, "seq", bit))
    got = beside(part_kv)
    half_kv = jnp.where(side == 0, jnp.stack([part_kv, got]), jnp.stack([got, part_kv]))
    quarters = gather_rows(half_kv)
    grad_kv = jnp.concatenate(
        [
            jnp.where(tp_index == j, quarters[0], jnp.where(tp_index == j ^ 1, quarters[1], jnp.where(tp_index == j ^ 2, quarters[2], quarters[3])))
            for j in range(tp_count)
        ]
    )
    grad_kv = jnp.swapaxes(grad_kv.astype(jnp.float32), 1, 2).reshape(dim, 2 * head_dim)

    grad_proj = exchange(done_p0, done_p1)
    sum_q = step_sum(sum_q, part_kv)
    sum_o = step_sum(sum_o, sum_q[0])
    done_f0 = finish_sum(sum_f0, sum_o[0])
    done_f1 = finish_sum(sum_f1, done_f0[0])
    done_q = finish_sum(sum_q, done_f1[0])
    done_o = finish_sum(sum_o, done_q[0])
    grad_fc = exchange(done_f0, done_f1).T
    grad_query = exchange(done_q).T
    grad_out_weight = exchange(done_o)
    return (
        layer_out,
        grad_in,
        shared[4 * dim : 5 * dim],
        shared[5 * dim : 6 * dim],
        grad_query,
        split[:queries_width],
        grad_kv,
        shared[6 * dim :],
        grad_out_weight,
        shared[3 * dim : 4 * dim],
        shared[dim : 2 * dim],
        shared[2 * dim : 3 * dim],
        grad_fc,
        split[queries_width:],
        grad_proj,
        shared[:dim],
    )


def solution(mesh):
    placed = (
        P(("seq", "tp"), None), P(), P(), P(), P(None, "tp"), P("tp"), P(), P(), P("tp", None),
        P(), P(), P(), P(None, "tp"), P("tp"), P("tp", None), P(), P(("seq", "tp"), None),
    )
    returned = (
        P(("seq", "tp"), None), P(("seq", "tp"), None), P(), P(), P("seq", "tp"), P("tp"), P(), P(),
        P("tp", "seq"), P(), P(), P(), P("seq", "tp"), P("tp"), P("tp", "seq"), P(),
    )
    return jax.shard_map(body, mesh=mesh, in_specs=placed, out_specs=returned, check_vma=False)
```

```python
import functools
import math

import jax
import jax.numpy as jnp
from jax import lax
from jax.experimental import pallas as pl
from jax.experimental.pallas import tpu as pltpu
from jax.sharding import PartitionSpec as P

EPS = 1e-05
NEG = -1e30
LOG2E = math.log2(math.e)
VMEM_LIMIT = 60 * 1024 * 1024
LIGHT = pl.CostEstimate(flops=1024, bytes_accessed=1024, transcendentals=0)
NT = (((1,), (1,)), ((), ()))


def dot(left, right):
    return jnp.dot(left, right, preferred_element_type=jnp.float32)


def dot_nt(left, right):
    return lax.dot_general(left, right, NT, preferred_element_type=jnp.float32)


def tie(value, *deps):
    return lax.optimization_barrier((value, *deps))[0]


def struct(shape, dtype):
    return jax.ShapeDtypeStruct(shape, dtype)


def swap(value, axis, bit):
    count = lax.axis_size(axis)
    return lax.ppermute(value, axis, [(j, j ^ bit) for j in range(count)])


def gather_rows(own):
    beside = swap(own, "tp", 1)
    across = swap(own, "tp", 2)
    return own, beside, across, swap(across, "tp", 1)


def touch_kernel(value, out):
    pass


def touch(value, *deps):
    anywhere = pl.BlockSpec(memory_space=pl.ANY)
    return pl.pallas_call(
        touch_kernel,
        in_specs=[anywhere],
        out_specs=anywhere,
        out_shape=struct(value.shape, value.dtype),
        input_output_aliases={0: 0},
        cost_estimate=LIGHT,
    )(tie(value, *deps))


def gather_pair(own):
    seq_count, tp_count = lax.axis_size("seq"), lax.axis_size("tp")
    wide = 2 * tp_count
    groups = [[first * wide + j for j in range(wide)] for first in range(seq_count // 2)]
    return lax.all_gather(own, ("seq", "tp"), axis=0, tiled=True, axis_index_groups=groups)


def half_gather(own):
    return own, swap(own, "tp", 1), swap(own, "tp", 2)


def full_gather(blocks, after):
    own, beside, across = blocks
    across = tie(across, after)
    return own, beside, across, swap(across, "tp", 1)


def call(kernel, outs, *args):
    return pl.pallas_call(
        kernel,
        out_shape=outs,
        compiler_params=pltpu.CompilerParams(vmem_limit_bytes=VMEM_LIMIT),
        cost_estimate=LIGHT,
    )(*args)


def total(*refs):
    return sum(ref[...].astype(jnp.float32) for ref in refs)


def add_kernel(*refs):
    refs[-1][...] = total(*refs[:-1]).astype(jnp.bfloat16)


def add_split_kernel(*refs):
    *parts, low_ref, high_ref = refs
    both = total(*parts).astype(jnp.bfloat16)
    half = low_ref.shape[0]
    low_ref[...] = both[:half]
    high_ref[...] = both[half:]


def add_split(*values):
    half = struct((values[0].shape[0] // 2, *values[0].shape[1:]), jnp.bfloat16)
    return call(add_split_kernel, [half, half], *values)


def columns_kernel(side, first, second, first_keep, second_keep, send):
    half = first_keep.shape[1]
    for index, (ref, keep) in enumerate(((first, first_keep), (second, second_keep))):
        low, high = ref[:, :half], ref[:, half:]
        keep[...] = jnp.where(side[0] == 0, low, high)
        send[:, index * half : (index + 1) * half] = jnp.where(side[0] == 0, high, low)


def add_low(*values):
    return call(add_kernel, struct(values[0].shape, jnp.bfloat16), *values)


def split_kernel(meta, keep_in, got_in, send_ref, keep_ref):
    both = total(keep_in, got_in).astype(jnp.bfloat16)

    @pl.when(pl.program_id(1) == 0)
    def _():
        send_ref[...] = both

    @pl.when(pl.program_id(1) == 1)
    def _():
        keep_ref[...] = both


def halves_kernel(side, *refs):
    *parts, mine, theirs = refs
    half = mine.shape[1]
    both = total(*parts).astype(jnp.bfloat16)
    low, high = both[:, :half], both[:, half:]
    mine[...] = jnp.where(side[0] == 0, low, high)
    theirs[...] = jnp.where(side[0] == 0, high, low)


def split_add(side, keep, got):
    parts, rows, columns = keep.shape
    block = pl.BlockSpec((1, rows, columns), lambda m, s, meta: (2 * m + (meta[0] + 1 - s) % 2, 0, 0))
    half = struct((parts // 2, rows, columns), jnp.bfloat16)
    return pl.pallas_call(
        split_kernel,
        grid_spec=pltpu.PrefetchScalarGridSpec(
            num_scalar_prefetch=1,
            grid=(parts // 2, 2),
            in_specs=[block, block],
            out_specs=[pl.BlockSpec((1, rows, columns), lambda m, s, meta: (m, 0, 0))] * 2,
        ),
        out_shape=[half, half],
        compiler_params=pltpu.CompilerParams(vmem_limit_bytes=VMEM_LIMIT),
        cost_estimate=LIGHT,
    )(jnp.stack([side]).astype(jnp.int32), keep, got)


def line_bits():
    bit = 2
    while bit < lax.axis_size("seq"):
        yield bit
        bit *= 2


def column_halves(value):
    side = lax.axis_index("seq") % 2
    half = value.shape[1] // 2
    keep = lax.dynamic_slice_in_dim(value, side * half, half, 1)
    send = lax.dynamic_slice_in_dim(value, (1 - side) * half, half, 1)
    return keep, send


def sum_over(value, axis):
    bit = 1
    while bit < lax.axis_size(axis):
        value = value + swap(value, axis, bit)
        bit *= 2
    return value


def normalized(features):
    centered = features - jnp.mean(features, axis=-1, keepdims=True)
    variance = jnp.mean(centered * centered, axis=-1, keepdims=True)
    scale = lax.rsqrt(variance + EPS)
    return centered * scale, scale


def norm_back(features, gain, grads):
    normed, scale = normalized(features)
    scaled = grads * gain
    mean = jnp.mean(scaled, axis=-1, keepdims=True)
    along = jnp.mean(scaled * normed, axis=-1, keepdims=True)
    over_rows = lambda value: jnp.sum(value, axis=0, keepdims=True)
    return scale * (scaled - mean - normed * along), over_rows(grads * normed), over_rows(grads)


def first_kernel(in_ref, gain, shift, w_ref, bias, norm_ref, key_ref, value_ref):
    normed, _ = normalized(in_ref[...].astype(jnp.float32))
    low = (normed * gain[...] + shift[...]).astype(jnp.bfloat16)
    norm_ref[...] = low
    pairs = dot(low, w_ref[...])
    hd = key_ref.shape[1]
    key_ref[...] = pairs[:, :hd].astype(jnp.bfloat16)
    value_ref[...] = (pairs[:, hd:] + bias[...]).astype(jnp.bfloat16)


def query_kernel(r0, r1, r2, r3, w_ref, bias, out_ref):
    rows = jnp.concatenate([r0[...], r1[...], r2[...], r3[...]], axis=0)
    out_ref[...] = (dot(rows, w_ref[...]) + bias[...]).astype(jnp.bfloat16)


def project_kernel(first, form, value_ref, w_ref, out0, out1):
    size = out0.shape[0]
    result = form(value_ref[first * size : (first + 2) * size, :], w_ref[...]).astype(jnp.bfloat16)
    out0[...] = result[:size]
    out1[...] = result[size:]


def middle_kernel(in_ref, p0, p1, p2, bias, gain, shift, middle_ref, norm_ref):
    middle = total(in_ref, p0, p1, p2) + bias[...]
    middle_ref[...] = middle
    normed, _ = normalized(middle)
    norm_ref[...] = (normed * gain[...] + shift[...]).astype(jnp.bfloat16)


def middle_back_kernel(middle_ref, p0, p1, p2, up_ref, gain, grads_ref, low_ref, sums_ref):
    upstream = up_ref[...].astype(jnp.float32)
    back, for_gain, for_shift = norm_back(middle_ref[...], gain[...], total(p0, p1, p2))
    grads = upstream + back
    grads_ref[...] = grads
    low_ref[...] = grads.astype(jnp.bfloat16)
    sums_ref[0:1] = jnp.sum(upstream, axis=0, keepdims=True)
    sums_ref[1:2] = for_gain
    sums_ref[2:3] = for_shift
    sums_ref[3:4] = jnp.sum(grads, axis=0, keepdims=True)


def attended_grads_kernel(r0, r1, r2, r3, w_ref, out_ref):
    rows = jnp.concatenate([r0[...], r1[...], r2[...], r3[...]], axis=0)
    out_ref[...] = dot_nt(rows, w_ref[...]).astype(jnp.bfloat16)


def layer_kernel(middle_ref, p0, p1, p2, bias, out_ref):
    out_ref[...] = (total(middle_ref, p0, p1, p2) + bias[...]).astype(jnp.bfloat16)


def last_kernel(in_ref, p0, p1, p2, pairs_ref, w_ref, middle_ref, gain, grads_ref, sums_ref, value_ref):
    hd = value_ref.shape[1]
    grads = total(p0, p1, p2) + dot_nt(pairs_ref[...], w_ref[...])
    back, for_gain, for_shift = norm_back(in_ref[...].astype(jnp.float32), gain[...], grads)
    grads_ref[...] = middle_ref[...] + back
    sums_ref[0:1] = for_gain
    sums_ref[1:2] = for_shift
    value_ref[...] = jnp.sum(pairs_ref[:, hd:].astype(jnp.float32), axis=0, keepdims=True)


def weight_kernel(counts, meta, *refs):
    terms, at = [], 0
    for count in counts:
        terms.append((refs[at : at + 8], refs[at + 8 : at + 8 + count]))
        at += 8 + count
    outs, token, scratch = refs[at : -len(counts) - 1], refs[-len(counts) - 1], refs[-len(counts) :]
    token[...] = jnp.zeros_like(token)

    @pl.when((pl.program_id(0) == 0) & (pl.program_id(1) == 0))
    def _():
        for (_, columns), turned in zip(terms, scratch):
            turn(columns, turned)

    start = 0
    for (rows, _), turned in zip(terms, scratch):
        joined = jnp.concatenate([ref[...] for ref in rows], axis=0)
        part = dot(turned[...], joined).astype(jnp.bfloat16)
        stop = start + part.shape[0]
        outs[0][0, start:stop] = part
        start = stop


def turn(refs, scratch):
    at = 0
    for ref in refs:
        scratch[:, at : at + ref.shape[0]] = ref[...].T
        at += ref.shape[0]


def block_width(rows):
    return (rows if isinstance(rows, jax.Array) else rows[0]).shape[1]


def row_blocks(rows, size, tile, column):
    if isinstance(rows, jax.Array):
        return [pl.BlockSpec((size, tile), lambda *ids, j=j: (ids[-1][2 + j], column(*ids))) for j in range(8)]
    return [pl.BlockSpec((size, tile), lambda *ids: (0, column(*ids)))] * 8


def weight_grads(meta, *terms):
    size, dim = terms[0][1][0].shape[0] * len(terms[0][1]) // 8, block_width(terms[0][0])
    parts = lax.axis_size("seq") // 2
    tile = dim // parts
    column = lambda m, s, meta: 2 * m + s
    specs, args, widths = [], [], []
    for rows, columns in terms:
        specs += row_blocks(rows, size, tile, column)
        specs += [pl.BlockSpec(value.shape, lambda m, s, meta: (0, 0)) for value in columns]
        args += [*([rows] * 8 if isinstance(rows, jax.Array) else rows), *columns]
        widths.append(columns[0].shape[1])
    out = (1, sum(widths), tile)
    out_specs = [
        pl.BlockSpec(out, lambda m, s, meta: (2 * m + s, 0, 0)),
        pl.BlockSpec((8, 128), lambda m, s, meta: (0, 0)),
    ]
    outs = [struct((parts, *out[1:]), jnp.bfloat16), struct((8, 128), jnp.float32)]
    return pl.pallas_call(
        functools.partial(weight_kernel, [len(columns) for _, columns in terms]),
        grid_spec=pltpu.PrefetchScalarGridSpec(
            num_scalar_prefetch=1,
            grid=(parts // 2, 2),
            in_specs=specs,
            out_specs=out_specs,
            scratch_shapes=[pltpu.VMEM((width, 8 * size), jnp.bfloat16) for width in widths],
        ),
        out_shape=outs,
        compiler_params=pltpu.CompilerParams(vmem_limit_bytes=VMEM_LIMIT),
        cost_estimate=LIGHT,
    )(meta, *args)


def slab_kernel(meta, *refs):
    *columns, out_ref, scratch = refs[8:]
    turn(columns, scratch)
    rows = jnp.concatenate([ref[...] for ref in refs[:8]], axis=0)
    out_ref[...] = dot(scratch[...], rows).astype(jnp.bfloat16)


def slab_grads(meta, rows, columns, parts):
    size = columns[0].shape[0] * len(columns) // 8
    tile = block_width(rows) // parts
    width = columns[0].shape[1]
    return pl.pallas_call(
        slab_kernel,
        grid_spec=pltpu.PrefetchScalarGridSpec(
            num_scalar_prefetch=1,
            grid=(1,),
            in_specs=row_blocks(rows, size, tile, lambda m, meta: meta[1])
            + [pl.BlockSpec(value.shape, lambda m, meta: (0, 0)) for value in columns],
            out_specs=pl.BlockSpec((width, tile), lambda m, meta: (0, 0)),
            scratch_shapes=[pltpu.VMEM((width, 8 * size), jnp.bfloat16)],
        ),
        out_shape=struct((width, tile), jnp.bfloat16),
        compiler_params=pltpu.CompilerParams(vmem_limit_bytes=VMEM_LIMIT),
        cost_estimate=LIGHT,
    )(meta, *([rows] * 8 if isinstance(rows, jax.Array) else rows), *columns)


def mlp_kernel(tiles, meta, x0, x1, g0, g1, fc_ref, proj_ref, bias_ref, *refs):
    a_send, a_keep, l_send, l_keep, m0, m1, t0, t1, sum_ref, x_ref, g_ref, macc, tacc = refs
    step = pl.program_id(0)
    size = x0.shape[0]

    @pl.when(step == 0)
    def _():
        x_ref[:size] = x0[...]
        x_ref[size:] = x1[...]
        g_ref[:size] = g0[...]
        g_ref[size:] = g1[...]

    values = dot(x_ref[...], fc_ref[...]) + bias_ref[...]
    grads = dot_nt(g_ref[...], proj_ref[...])
    root = math.sqrt(2 / math.pi)
    square = values * values
    bend = jnp.tanh(root * values * (1 + 0.044715 * square))
    half = 0.5 * (1 + bend)
    slope = half + 0.5 * root * values * (1 - bend * bend) * (1 + 3 * 0.044715 * square)
    activated = (values * half).astype(jnp.bfloat16)
    grads = grads * slope
    sum_ref[...] = jnp.sum(grads, axis=0, keepdims=True)
    low = grads.astype(jnp.bfloat16)

    @pl.when(step == 0)
    def _():
        macc[...] = jnp.zeros_like(macc)
        tacc[...] = jnp.zeros_like(tacc)

    chunk = macc.shape[1] // 4
    for c in range(4):
        cut = slice(c * chunk, (c + 1) * chunk)
        macc[:, cut] += dot(activated, proj_ref[:, cut])
        tacc[:, cut] += dot_nt(low, fc_ref[cut, :])

    @pl.when(step < tiles // 2)
    def _():
        a_send[...] = activated
        l_send[...] = low

    @pl.when(step >= tiles // 2)
    def _():
        a_keep[...] = activated
        l_keep[...] = low

    @pl.when(step == tiles - 1)
    def _():
        f = macc[...].astype(jnp.bfloat16)
        b = tacc[...].astype(jnp.bfloat16)
        m0[...] = f[:size]
        m1[...] = f[size:]
        t0[...] = b[:size]
        t1[...] = b[size:]


def mlp(blocks, ups, meta, w_fc, w_proj, b_fc):
    size, dim = blocks[0].shape
    hidden = w_fc.shape[1]
    tiles = 4
    width = hidden // tiles
    tile = lambda n, meta: ((n // (tiles // 2)) ^ (1 - meta[10])) * (tiles // 2) + n % (tiles // 2)
    fixed = pl.BlockSpec((size, dim), lambda n, meta: (0, 0))
    columns = lambda start: pl.BlockSpec(
        (2 * size, width), lambda n, meta: (0, jnp.clip(n - start, 0, tiles // 2 - 1))
    )
    half = struct((2 * size, hidden // 2), jnp.bfloat16)
    rows = struct((size, dim), jnp.bfloat16)
    return pl.pallas_call(
        functools.partial(mlp_kernel, tiles),
        grid_spec=pltpu.PrefetchScalarGridSpec(
            num_scalar_prefetch=1,
            grid=(tiles,),
            in_specs=[fixed] * 4
            + [
                pl.BlockSpec((dim, width), lambda n, meta: (0, tile(n, meta))),
                pl.BlockSpec((width, dim), lambda n, meta: (tile(n, meta), 0)),
                pl.BlockSpec((1, width), lambda n, meta: (0, tile(n, meta))),
            ],
            out_specs=[columns(0), columns(tiles // 2)] * 2
            + [fixed] * 4
            + [pl.BlockSpec((1, width), lambda n, meta: (0, tile(n, meta)))],
            scratch_shapes=[pltpu.VMEM((2 * size, dim), jnp.bfloat16)] * 2 + [pltpu.VMEM((2 * size, dim), jnp.float32)] * 2,
        ),
        out_shape=[half] * 4 + [rows] * 4 + [struct((1, hidden), jnp.float32)],
        compiler_params=pltpu.CompilerParams(vmem_limit_bytes=VMEM_LIMIT),
        cost_estimate=LIGHT,
    )(meta, *blocks, *ups, w_fc, w_proj, b_fc[None, :])


def allowed_pairs(slot, masks_ref, rows_ref, keys_ref):
    place = keys_ref[...] + masks_ref[2, slot]
    return (place <= rows_ref[0:1, :]) & (place >= rows_ref[1:2, :])


def when_live(meta, slot, visit):
    @pl.when((meta[0, slot] == 1) & (meta[1, slot] == 0))
    def _():
        visit(True)

    @pl.when((meta[0, slot] == 1) & (meta[1, slot] == 1))
    def _():
        visit(False)


def forward_kernel(heads, meta, q_ref, *refs):
    key_refs, value_refs = refs[:4], refs[4:8]
    rows_ref, keys_ref, out_ref, norm_ref, m_ref, l_ref, acc_ref = refs[8:]
    hd = q_ref.shape[1] // heads
    scale = hd ** (-0.5) * LOG2E
    slots = key_refs[0].shape[0]

    def visit(slot, masked, exact):
        keys = jnp.concatenate([ref[slot] for ref in key_refs], axis=0)
        values_t = jnp.concatenate([ref[slot] for ref in value_refs], axis=0).T
        if masked:
            allowed = allowed_pairs(slot, meta, rows_ref, keys_ref)
        for h in range(heads):
            scores = dot_nt(keys, q_ref[:, h * hd : (h + 1) * hd]) * scale
            if masked:
                scores = jnp.where(allowed, scores, NEG)
            top = m_ref[h : h + 1, :]
            if exact:
                new = jnp.maximum(top, jnp.max(scores, axis=0, keepdims=True))
                decay = jnp.exp2(top - new)
                m_ref[h : h + 1, :] = new
                l_ref[h : h + 1, :] = l_ref[h : h + 1, :] * decay
                acc_ref[h] = acc_ref[h] * decay
                top = new
            weights = jnp.exp2(scores - top)
            l_ref[h : h + 1, :] += jnp.sum(weights, axis=0, keepdims=True)
            acc_ref[h] += dot(values_t, weights.astype(jnp.bfloat16))

    def run(exact):
        m_ref[...] = jnp.full_like(m_ref, NEG)
        l_ref[...] = jnp.zeros_like(l_ref)
        acc_ref[...] = jnp.zeros_like(acc_ref)
        visit(0, True, True)

        def body(slot, carry):
            when_live(meta, slot, lambda masked: visit(slot, masked, exact))
            return carry

        lax.fori_loop(1, slots, body, 0)

    run(False)

    @pl.when(jnp.logical_not(jnp.max(l_ref[...]) < 2.0**100))
    def _():
        run(True)

    norm_ref[...] = m_ref[...] + jnp.log2(l_ref[...])
    for h in range(heads):
        result = acc_ref[h] / l_ref[h : h + 1, :]
        out_ref[:, h * hd : (h + 1) * hd] = result.T.astype(jnp.bfloat16)


def backward_visit(heads, slot, meta, q_ref, key_refs, value_refs, rows_ref, keys_ref, norm_ref, up_ref, delta_ref, dq_acc, d_refs):
    hd = q_ref.shape[1] // heads
    part = key_refs[0].shape[1]
    scale = hd ** (-0.5)

    def visit(masked):
        keys = jnp.concatenate([ref[0] for ref in key_refs], axis=0)
        values = jnp.concatenate([ref[0] for ref in value_refs], axis=0)
        keys_t = keys.T
        if masked:
            allowed = allowed_pairs(slot, meta, rows_ref, keys_ref)
        dk = dv = None
        for h in range(heads):
            q = q_ref[:, h * hd : (h + 1) * hd]
            up = up_ref[:, h * hd : (h + 1) * hd]
            weights = jnp.exp2(dot_nt(keys, q) * (scale * LOG2E) - norm_ref[h : h + 1, :])
            if masked:
                weights = jnp.where(allowed, weights, 0.0)
            grads = dot_nt(values, up)
            score_grads = (weights * (grads - delta_ref[h : h + 1, :])).astype(jnp.bfloat16)
            dv_h = dot(weights.astype(jnp.bfloat16), up)
            dk_h = dot(score_grads, q)
            dv = dv_h if dv is None else dv + dv_h
            dk = dk_h if dk is None else dk + dk_h
            dq_acc[h] = dq_acc[h] + dot(keys_t, score_grads)
        for index, ref in enumerate(d_refs):
            part_rows = slice(index * part, (index + 1) * part)
            ref[0, :, :hd] = (dk[part_rows] * scale).astype(jnp.bfloat16)
            ref[0, :, hd:] = dv[part_rows].astype(jnp.bfloat16)

    @pl.when(meta[0, slot] == 0)
    def _():
        for ref in d_refs:
            ref[...] = jnp.zeros_like(ref)

    when_live(meta, slot, visit)


def backward_first_kernel(heads, first, meta, q_ref, *refs):
    key_refs, value_refs = refs[:4], refs[4:8]
    rows_ref, keys_ref, norm_ref, up_ref, att_ref, acc_ref, delta_ref = refs[8:15]
    d_refs = refs[15:19]
    hd = q_ref.shape[1] // heads

    @pl.when(pl.program_id(0) == 0)
    def _():
        acc_ref[...] = jnp.zeros_like(acc_ref)
        for h in range(heads):
            cols = slice(h * hd, (h + 1) * hd)
            both = att_ref[:, cols].astype(jnp.float32) * up_ref[:, cols].astype(jnp.float32)
            delta_ref[h : h + 1, :] = jnp.sum(both.T, axis=0, keepdims=True)

    slot = pl.program_id(0) + first
    backward_visit(heads, slot, meta, q_ref, key_refs, value_refs, rows_ref, keys_ref, norm_ref, up_ref, delta_ref, acc_ref, d_refs)


def backward_last_kernel(heads, first, meta, q_ref, *refs):
    key_refs, value_refs = refs[:4], refs[4:8]
    rows_ref, keys_ref, norm_ref, up_ref, start_ref, delta_ref, dq_ref, bias_ref = refs[8:16]
    d_refs = refs[16:20]
    acc_ref = refs[20]
    hd = q_ref.shape[1] // heads

    @pl.when(pl.program_id(0) == 0)
    def _():
        acc_ref[...] = start_ref[...]

    slot = pl.program_id(0) + first
    backward_visit(heads, slot, meta, q_ref, key_refs, value_refs, rows_ref, keys_ref, norm_ref, up_ref, delta_ref, acc_ref, d_refs)

    @pl.when(pl.program_id(0) == pl.num_programs(0) - 1)
    def _():
        for h in range(heads):
            result = (acc_ref[h] * hd ** (-0.5)).T
            bias_ref[:, h * hd : (h + 1) * hd] = jnp.sum(result, axis=0, keepdims=True)
            dq_ref[:, h * hd : (h + 1) * hd] = result.astype(jnp.bfloat16)


def whole(value):
    return pl.BlockSpec(value.shape, lambda step, meta: (0,) * len(value.shape))


def attention_call(kernel, meta, first, steps, slots, queries, keys, values, extra, outs, scratch, passes):
    rows, width = queries.shape
    part, hd = keys[0].shape[1:]
    block = lambda columns, start: pl.BlockSpec((slots // steps, part, columns), lambda step, meta: (step + start, 0, 0))
    heads = width // hd
    return pl.pallas_call(
        kernel,
        grid_spec=pltpu.PrefetchScalarGridSpec(
            num_scalar_prefetch=1,
            grid=(steps,),
            in_specs=[whole(queries)] + [block(hd, first)] * 8 + [whole(value) for value in extra],
            out_specs=[block(2 * hd, 0) if out.shape == (slots, part, 2 * hd) else whole(out) for out in outs],
            scratch_shapes=scratch,
        ),
        out_shape=outs,
        compiler_params=pltpu.CompilerParams(vmem_limit_bytes=VMEM_LIMIT),
        cost_estimate=LIGHT,
    )(meta, queries, *keys, *values, *extra)


def attention_forward(queries, keys, values, meta, rows_info, keys_info, heads):
    rows, width = queries.shape
    return attention_call(
        functools.partial(forward_kernel, heads), meta, 0, 1, keys[0].shape[0], queries, keys, values,
        [rows_info, keys_info],
        [struct((rows, width), jnp.bfloat16), struct((heads, rows), jnp.float32)],
        [
            pltpu.VMEM((heads, rows), jnp.float32),
            pltpu.VMEM((heads, rows), jnp.float32),
            pltpu.VMEM((heads, width // heads, rows), jnp.float32),
        ],
        2,
    )


def backward_calls(queries, keys, values, meta, rows_info, keys_info, norm, attended, upstream, heads):
    rows, width = queries.shape
    hd = width // heads
    n, part = keys[0].shape[:2]
    half = n // 2
    grads = [struct((half, part, 2 * hd), jnp.bfloat16)] * 4
    shared = [rows_info, keys_info, norm, upstream]

    def first(*deps):
        return attention_call(
            functools.partial(backward_first_kernel, heads, half), meta, half, half, half, tie(queries, *deps),
            keys, values, shared + [attended],
            [struct((heads, hd, rows), jnp.float32), struct((heads, rows), jnp.float32)] + grads,
            [], 5,
        )

    def last(start, delta, *deps):
        return attention_call(
            functools.partial(backward_last_kernel, heads, 0), meta, 0, half, half, tie(queries, *deps),
            keys, values, shared + [start, delta],
            [struct((rows, width), jnp.bfloat16), struct((1, width), jnp.float32)] + grads,
            [pltpu.VMEM((heads, hd, rows), jnp.float32)], 5,
        )

    return first, last


def gather_slots(own, bits, axis):
    found = {0: own}
    for bit in bits:
        masks = sorted(found)
        stacked = jnp.stack([found[m] for m in masks])
        got = swap(stacked, axis, bit)
        found.update({m ^ bit: got[j] for j, m in enumerate(masks)})
    return found


def body(
    hidden_in, lengths, ln1_gain, ln1_bias, w_query, b_query, w_kv, b_value, w_out, b_out,
    ln2_gain, ln2_bias, w_fc, b_fc, w_proj, b_proj, grad_out,
):
    seq_count = lax.axis_size("seq")
    tp_count = lax.axis_size("tp")
    seq_index = lax.axis_index("seq")
    tp_index = lax.axis_index("tp")
    own_rows, dim = hidden_in.shape
    group_rows = own_rows * tp_count
    head_dim = b_value.shape[0]
    heads = w_query.shape[1] // head_dim
    joined = lambda *blocks: jnp.concatenate(blocks, axis=0)
    seq_bits = [1 << j for j in range(seq_count.bit_length() - 1)]

    order = jnp.stack([tp_index, tp_index ^ 1, tp_index ^ 2, tp_index ^ 3]).astype(jnp.int32)
    inside = (order[:, None] * own_rows + jnp.arange(own_rows, dtype=jnp.int32)[None, :]).reshape(-1)
    group_first = seq_index * group_rows
    doc_ends = jnp.cumsum(lengths)
    begins = jnp.max(
        jnp.where(doc_ends[None, :] <= (inside + group_first)[:, None], doc_ends[None, :], 0), axis=1
    )
    rows_info = jnp.stack([inside, begins - group_first])
    keys_info = inside[:, None]
    slot_group = seq_index ^ jnp.arange(seq_count, dtype=jnp.int32)
    key_first = slot_group * group_rows
    live = (slot_group <= seq_index) & (key_first + group_rows > jnp.min(begins))
    clear = (slot_group < seq_index) & (key_first >= jnp.max(begins))
    meta = jnp.stack([live, clear, key_first - group_first]).astype(jnp.int32)
    side = seq_index % 2
    scalar = lambda value: jnp.stack([value]).astype(jnp.int32)
    side_scalar = scalar(side)
    places = [scalar((seq_index // 2) % 2), scalar(2 * tp_index + side)]
    places = jnp.concatenate(places + [side * tp_count + order, (1 - side) * tp_count + order, scalar(side)])
    beside = lambda value: swap(value, "seq", 1)

    row = lambda vector: vector[None, :]
    rows_low = struct((own_rows, dim), jnp.bfloat16)
    rows_wide = struct((own_rows, dim), jnp.float32)
    narrow = struct((own_rows, head_dim), jnp.bfloat16)
    normed_one, key_own, value_own = call(
        first_kernel, [rows_low, narrow, narrow], hidden_in, row(ln1_gain), row(ln1_bias), w_kv, row(b_value)
    )
    key_slots = gather_slots(key_own, seq_bits[::-1], "seq")
    key_stack = jnp.stack([key_slots[m] for m in range(seq_count)])
    value_two = jnp.stack([value_own, swap(value_own, "tp", 2)])
    value_slots = gather_slots(value_two, seq_bits[::-1], "seq")
    value_two = jnp.stack([value_slots[m] for m in range(seq_count)], axis=1)
    value_beside = swap(value_two, "tp", 1)
    values = [value_two[0], value_beside[0], value_two[1], value_beside[1]]
    blocks_one = gather_rows(normed_one)
    queries = call(
        query_kernel, struct((group_rows, heads * head_dim), jnp.bfloat16), *blocks_one, w_query, row(b_query)
    )
    key_across = tie(swap(key_stack, "tp", 2), queries)
    keys = [key_stack, swap(key_stack, "tp", 1), key_across, swap(key_across, "tp", 1)]
    ups_own = gather_rows(tie(grad_out, queries))
    up_other, one_other = beside(tie(grad_out, queries)), beside(tie(normed_one, queries))
    attended, norm = attention_forward(queries, keys, values, meta, rows_info, keys_info, heads)

    def project(value, weight, form):
        far = call(functools.partial(project_kernel, 2, form), [rows_low] * 2, value, weight)
        near = call(functools.partial(project_kernel, 0, form), [rows_low] * 2, tie(value, far[0]), weight)
        return (*near, *far)

    def scatter(own, beside, across, opposite, *deps):
        over = add_low(tie(across, *deps), swap(opposite, "tp", 1))
        return own, swap(beside, "tp", 1), over, swap(over, "tp", 2)

    att0, att1, _, att2 = scatter(*project(attended, w_out, dot))
    middle, normed_two = call(
        middle_kernel, [rows_wide, rows_low], hidden_in, att0, att1, att2, row(b_out), row(ln2_gain), row(ln2_bias)
    )

    two_beside, two_across = swap(normed_two, "tp", 1), swap(normed_two, "tp", 2)
    two_other = beside(normed_two)
    act_send0, act_keep0, low_send0, low_keep0, mlp0, mlp1, two0, two1, sum_near = mlp(
        (normed_two, tie(two_beside, up_other, one_other)), ups_own[:2], places, w_fc, w_proj, b_fc
    )
    two_across = tie(two_across, two0)
    two_opposite = swap(two_across, "tp", 1)
    ups_other = half_gather(tie(up_other, two0))
    act_other0 = beside(act_send0)
    act_send1, act_keep1, low_send1, low_keep1, mlp2, mlp3, two2, two3, sum_far = mlp(
        (two_across, two_opposite), ups_own[2:], places, w_fc, w_proj, b_fc
    )

    line = list(line_bits())
    line_side = lambda bit: (seq_index // bit) % 2

    def group_sum(parts):
        groups = [list(range(first, seq_count, 2)) for first in range(2)]
        flat = parts.reshape(-1, parts.shape[2])
        return lax.psum_scatter(flat, "seq", scatter_dimension=0, tiled=True, axis_index_groups=groups)

    def step_sum(state, *deps):
        keep, got, bits = state
        if not bits:
            return state
        keep = tie(keep, *deps)
        send, kept = split_add(line_side(bits[0]), keep, got)
        return kept, swap(send, "seq", bits[0]), bits[1:]

    def halves(*parts):
        rows, columns = parts[0].shape
        return pl.pallas_call(
            halves_kernel,
            in_specs=[pl.BlockSpec(memory_space=pltpu.SMEM)] + [pl.BlockSpec((rows, columns))] * len(parts),
            out_shape=[struct((rows, columns // 2), jnp.bfloat16)] * 2,
            compiler_params=pltpu.CompilerParams(vmem_limit_bytes=VMEM_LIMIT),
            cost_estimate=LIGHT,
        )(side_scalar, *parts)

    def exchange(mine, theirs):
        both = [jnp.where(side == 0, mine, theirs), jnp.where(side == 0, theirs, mine)]
        return joined(*both).astype(jnp.float32)

    act_other1 = beside(act_send1)

    clock = [two2]

    def at(value, *arrived):
        return tie(value, clock[0], *arrived)

    def mark(results):
        clock[0] = results[0] if isinstance(results, (list, tuple)) else results
        return results

    core = lambda value: swap(value, "tp", 1)
    chip = lambda value: swap(value, "tp", 2)

    two_over = mark(add_low(at(two2, act_other0, two_other, ups_other[2]), core(two3)))
    two_own, two_got = core(two1), chip(two_over)
    middle_grads, middle_low, sums_two = mark(
        call(
            middle_back_kernel,
            [rows_wide, rows_low, struct((4, dim), jnp.float32)],
            middle, two0, two_own, two_got, grad_out, at(row(ln2_gain)),
        )
    )
    mid_beside, mid_across = core(middle_low), chip(middle_low)
    low_other0, low_other1 = beside(at(low_send0)), beside(at(low_send1))
    ups = ups_own + full_gather(ups_other, middle_low)
    part_p, clock[0] = weight_grads(places, (ups, (at(act_keep0), act_keep1, act_other0, act_other1)))
    mid_opposite = core(at(mid_across))
    mids_own = (middle_low, mid_beside, mid_across, mid_opposite)

    attended_grads = mark(
        call(attended_grads_kernel, struct(attended.shape, jnp.bfloat16), *mids_own, at(w_out))
    )
    sum_p = group_sum(touch(part_p, mid_across))
    twos_other = half_gather(at(two_other))
    ones_other = half_gather(at(one_other))
    first_call, last_call = backward_calls(
        queries, keys, values, meta, rows_info, keys_info, norm, attended, attended_grads, heads
    )
    start, delta, *kv_far = mark(first_call(attended_grads))
    mid_other = beside(at(middle_low))
    far_over = mark(add_low(at(kv_far[2], low_other0, low_other1, twos_other[2]), core(kv_far[3])))
    twos = (normed_two, two_beside, two_across, two_opposite) + full_gather(twos_other, far_over)
    far_own, far_got = core(kv_far[1]), chip(far_over)
    query_low, bias_query, *kv_near = mark(last_call(start, delta, far_over))

    one2, one3 = mark(
        call(
            functools.partial(project_kernel, 2, dot_nt), [rows_low] * 2,
            at(query_low, far_got, far_own, mid_other, ones_other[2]), w_query,
        )
    )
    ones = blocks_one + full_gather(ones_other, one2)
    near_over = mark(add_low(at(kv_near[2]), core(kv_near[3])))
    mid_others = mid_other, core(at(mid_other)), chip(at(mid_other))
    near_own, near_got = core(kv_near[1]), chip(near_over)
    far_sum = mark(add_low(at(kv_far[0]), far_own, far_got))
    far_there = swap(far_sum, "seq", seq_count // 2)
    one_over = mark(add_low(at(one2), core(one3)))
    one_got = chip(one_over)
    part = struct((group_rows, heads * head_dim // 2), jnp.bfloat16)
    dq_keep, att_keep, sends = mark(
        pl.pallas_call(
            columns_kernel,
            in_specs=[pl.BlockSpec(memory_space=pltpu.SMEM)] + [pl.BlockSpec(query_low.shape)] * 2,
            out_shape=[part, part, struct(query_low.shape, jnp.bfloat16)],
            compiler_params=pltpu.CompilerParams(vmem_limit_bytes=VMEM_LIMIT),
            cost_estimate=LIGHT,
        )(side_scalar, at(query_low), attended)
    )
    others = beside(sends)
    part_f, clock[0] = weight_grads(places, (twos, (at(low_keep0), low_keep1, low_other0, low_other1)))
    kv_slots, there = mark(add_split(at(kv_near[0], others, mid_others[2]), near_own, near_got, far_there))
    sum_f = group_sum(touch(part_f, far_there))
    there = swap(there, "seq", seq_bits[-2])
    mid_others = (*mid_others, core(at(mid_others[2])))
    one0, one1 = mark(
        call(functools.partial(project_kernel, 0, dot_nt), [rows_low] * 2, at(query_low), w_query)
    )
    one_own = core(one1)
    width = dq_keep.shape[1]
    part_qo, clock[0] = weight_grads(
        places,
        (ones, (at(dq_keep), others[:, :width])),
        (mids_own + mid_others, (att_keep, others[:, width:])),
    )
    for bit in seq_bits[-3::-1]:
        kv_slots, send = mark(add_split(at(kv_slots), there))
        there = swap(send, "seq", bit)
    kv_low = mark(add_low(at(kv_slots, one_got), there))[0]
    kv_beside, kv_across = core(kv_low), chip(kv_low)
    sum_qo = group_sum(touch(part_qo, kv_low))
    grad_in, sums_one, sums_value = mark(
        call(
            last_kernel,
            [rows_wide, struct((2, dim), jnp.float32), struct((1, head_dim), jnp.float32)],
            hidden_in, one0, one_own, one_got, kv_low, w_kv, middle_grads, at(row(ln1_gain)),
        )
    )

    count = 6 * dim + head_dim
    vectors = [sums_two.reshape(-1), sums_one.reshape(-1), sums_value[0], bias_query[0], (sum_near + sum_far)[0]]
    vectors = jnp.concatenate(vectors).reshape(-1, 128)
    got = swap(vectors, "seq", seq_bits[1])
    kv_group = joined(kv_low, kv_beside, kv_across, core(at(kv_across)))
    kv_other = beside(kv_group)
    mine_p, theirs_p = mark(halves(at(sum_p)))
    theirs_p = beside(theirs_p)
    mlp_over = mark(add_low(at(mlp2), core(at(mlp3))))
    mlp_own, mlp_got = core(at(mlp1)), chip(mlp_over)
    vectors = vectors + at(got)
    got = swap(vectors, "seq", seq_bits[2])
    part_kv = mark(slab_grads(places, ones, (at(kv_group), kv_other), 2 * tp_count))
    got_kv = swap(part_kv, "seq", seq_bits[1])
    vectors = vectors + at(got)
    for bit in seq_bits[2:]:
        part_kv = mark(add_low(at(part_kv), got_kv))
        got_kv = swap(part_kv, "seq", bit)
    for bit in seq_bits[3:]:
        vectors = vectors + swap(vectors, "seq", bit)
    got = swap(vectors, "seq", 1)
    part_kv = mark(add_low(at(part_kv), got_kv))
    got_kv = beside(part_kv)
    layer_out = mark(call(layer_kernel, rows_low, at(middle), mlp0, mlp_own, mlp_got, row(b_proj)))
    vectors = (vectors + at(got)).reshape(-1)
    shared, split = vectors[:count].reshape(-1, 128), vectors[count:]
    got = chip(shared)
    grad_proj = exchange(at(mine_p), theirs_p)
    half_kv = jnp.where(side == 0, jnp.stack([part_kv, got_kv]), jnp.stack([got_kv, part_kv]))
    half_beside, half_across = core(half_kv), chip(half_kv)
    mine_f, theirs_f = mark(halves(tie(sum_f, half_kv)))
    theirs_f = beside(theirs_f)
    shared = shared + at(got)
    got = core(shared)
    half_opposite = core(at(half_across))
    shared = (shared + at(got)).reshape(-1)
    grad_fc = exchange(at(mine_f), theirs_f).T
    quarters = half_kv, half_beside, half_across, half_opposite
    grad_kv = jnp.concatenate(
        [
            jnp.where(tp_index == j, quarters[0], jnp.where(tp_index == j ^ 1, quarters[1], jnp.where(tp_index == j ^ 2, quarters[2], quarters[3])))
            for j in range(tp_count)
        ]
    )
    grad_kv = jnp.swapaxes(grad_kv.astype(jnp.float32), 1, 2).reshape(dim, 2 * head_dim)
    mine_qo, theirs_qo = mark(halves(tie(sum_qo, grad_fc, grad_kv, shared)))
    theirs_qo = beside(theirs_qo)
    grad_query = exchange(mine_qo[:width], theirs_qo[:width]).T
    grad_out_weight = exchange(mine_qo[width:], theirs_qo[width:])
    queries_width = bias_query.shape[1]
    return (
        layer_out,
        grad_in,
        shared[4 * dim : 5 * dim],
        shared[5 * dim : 6 * dim],
        grad_query,
        split[:queries_width],
        grad_kv,
        shared[6 * dim :],
        grad_out_weight,
        shared[3 * dim : 4 * dim],
        shared[dim : 2 * dim],
        shared[2 * dim : 3 * dim],
        grad_fc,
        split[queries_width:],
        grad_proj,
        shared[:dim],
    )


def solution(mesh):
    placed = (
        P(("seq", "tp"), None), P(), P(), P(), P(None, "tp"), P("tp"), P(), P(), P("tp", None),
        P(), P(), P(), P(None, "tp"), P("tp"), P("tp", None), P(), P(("seq", "tp"), None),
    )
    returned = (
        P(("seq", "tp"), None), P(("seq", "tp"), None), P(), P(), P("seq", "tp"), P("tp"), P(), P(),
        P("tp", "seq"), P(), P(), P(), P("seq", "tp"), P("tp"), P("tp", "seq"), P(),
    )
    return jax.shard_map(body, mesh=mesh, in_specs=placed, out_specs=returned, check_vma=False)
```

```python
import functools
import math

import jax
import jax.numpy as jnp
from jax import lax
from jax.experimental import pallas as pl
from jax.experimental.pallas import tpu as pltpu
from jax.sharding import PartitionSpec as P

EPS = 1e-05
NEG = -1e30
LOG2E = math.log2(math.e)
VMEM_LIMIT = 60 * 1024 * 1024
LIGHT = pl.CostEstimate(flops=1024, bytes_accessed=1024, transcendentals=0)
NT = (((1,), (1,)), ((), ()))


def dot(left, right):
    return jnp.dot(left, right, preferred_element_type=jnp.float32)


def dot_nt(left, right):
    return lax.dot_general(left, right, NT, preferred_element_type=jnp.float32)


def tie(value, *deps):
    return lax.optimization_barrier((value, *deps))[0]


def struct(shape, dtype):
    return jax.ShapeDtypeStruct(shape, dtype)


def swap(value, axis, bit):
    count = lax.axis_size(axis)
    return lax.ppermute(value, axis, [(j, j ^ bit) for j in range(count)])


def gather_rows(own):
    beside = swap(own, "tp", 1)
    across = swap(own, "tp", 2)
    return own, beside, across, swap(across, "tp", 1)


def touch_kernel(value, out):
    pass


def touch(value, *deps):
    anywhere = pl.BlockSpec(memory_space=pl.ANY)
    return pl.pallas_call(
        touch_kernel,
        in_specs=[anywhere],
        out_specs=anywhere,
        out_shape=struct(value.shape, value.dtype),
        input_output_aliases={0: 0},
        cost_estimate=LIGHT,
    )(tie(value, *deps))


def gather_pair(own):
    seq_count, tp_count = lax.axis_size("seq"), lax.axis_size("tp")
    wide = 2 * tp_count
    groups = [[first * wide + j for j in range(wide)] for first in range(seq_count // 2)]
    return lax.all_gather(own, ("seq", "tp"), axis=0, tiled=True, axis_index_groups=groups)


def half_gather(own):
    return own, swap(own, "tp", 1), swap(own, "tp", 2)


def full_gather(blocks, after):
    own, beside, across = blocks
    across = tie(across, after)
    return own, beside, across, swap(across, "tp", 1)


def call(kernel, outs, *args):
    return pl.pallas_call(
        kernel,
        out_shape=outs,
        compiler_params=pltpu.CompilerParams(vmem_limit_bytes=VMEM_LIMIT),
        cost_estimate=LIGHT,
    )(*args)


def total(*refs):
    return sum(ref[...].astype(jnp.float32) for ref in refs)


def add_kernel(*refs):
    refs[-1][...] = total(*refs[:-1]).astype(jnp.bfloat16)


def add_split_kernel(*refs):
    *parts, low_ref, high_ref = refs
    both = total(*parts).astype(jnp.bfloat16)
    half = low_ref.shape[0]
    low_ref[...] = both[:half]
    high_ref[...] = both[half:]


def add_split(*values):
    half = struct((values[0].shape[0] // 2, *values[0].shape[1:]), jnp.bfloat16)
    return call(add_split_kernel, [half, half], *values)


def columns_kernel(side, first, second, first_keep, second_keep, send):
    half = first_keep.shape[1]
    for index, (ref, keep) in enumerate(((first, first_keep), (second, second_keep))):
        low, high = ref[:, :half], ref[:, half:]
        keep[...] = jnp.where(side[0] == 0, low, high)
        send[:, index * half : (index + 1) * half] = jnp.where(side[0] == 0, high, low)


def add_low(*values):
    return call(add_kernel, struct(values[0].shape, jnp.bfloat16), *values)


def split_kernel(meta, keep_in, got_in, send_ref, keep_ref):
    both = total(keep_in, got_in).astype(jnp.bfloat16)

    @pl.when(pl.program_id(1) == 0)
    def _():
        send_ref[...] = both

    @pl.when(pl.program_id(1) == 1)
    def _():
        keep_ref[...] = both


def halves_kernel(side, *refs):
    *parts, mine, theirs = refs
    half = mine.shape[1]
    both = total(*parts).astype(jnp.bfloat16)
    low, high = both[:, :half], both[:, half:]
    mine[...] = jnp.where(side[0] == 0, low, high)
    theirs[...] = jnp.where(side[0] == 0, high, low)


def split_add(side, keep, got):
    parts, rows, columns = keep.shape
    block = pl.BlockSpec((1, rows, columns), lambda m, s, meta: (2 * m + (meta[0] + 1 - s) % 2, 0, 0))
    half = struct((parts // 2, rows, columns), jnp.bfloat16)
    return pl.pallas_call(
        split_kernel,
        grid_spec=pltpu.PrefetchScalarGridSpec(
            num_scalar_prefetch=1,
            grid=(parts // 2, 2),
            in_specs=[block, block],
            out_specs=[pl.BlockSpec((1, rows, columns), lambda m, s, meta: (m, 0, 0))] * 2,
        ),
        out_shape=[half, half],
        compiler_params=pltpu.CompilerParams(vmem_limit_bytes=VMEM_LIMIT),
        cost_estimate=LIGHT,
    )(jnp.stack([side]).astype(jnp.int32), keep, got)


def line_bits():
    bit = 2
    while bit < lax.axis_size("seq"):
        yield bit
        bit *= 2


def column_halves(value):
    side = lax.axis_index("seq") % 2
    half = value.shape[1] // 2
    keep = lax.dynamic_slice_in_dim(value, side * half, half, 1)
    send = lax.dynamic_slice_in_dim(value, (1 - side) * half, half, 1)
    return keep, send


def sum_over(value, axis):
    bit = 1
    while bit < lax.axis_size(axis):
        value = value + swap(value, axis, bit)
        bit *= 2
    return value


def normalized(features):
    centered = features - jnp.mean(features, axis=-1, keepdims=True)
    variance = jnp.mean(centered * centered, axis=-1, keepdims=True)
    scale = lax.rsqrt(variance + EPS)
    return centered * scale, scale


def norm_back(features, gain, grads):
    normed, scale = normalized(features)
    scaled = grads * gain
    mean = jnp.mean(scaled, axis=-1, keepdims=True)
    along = jnp.mean(scaled * normed, axis=-1, keepdims=True)
    over_rows = lambda value: jnp.sum(value, axis=0, keepdims=True)
    return scale * (scaled - mean - normed * along), over_rows(grads * normed), over_rows(grads)


def first_kernel(in_ref, gain, shift, w_ref, bias, norm_ref, key_ref, value_ref):
    normed, _ = normalized(in_ref[...].astype(jnp.float32))
    low = (normed * gain[...] + shift[...]).astype(jnp.bfloat16)
    norm_ref[...] = low
    pairs = dot(low, w_ref[...])
    hd = key_ref.shape[1]
    key_ref[...] = pairs[:, :hd].astype(jnp.bfloat16)
    value_ref[...] = (pairs[:, hd:] + bias[...]).astype(jnp.bfloat16)


def query_kernel(r0, r1, r2, r3, w_ref, bias, out_ref):
    rows = jnp.concatenate([r0[...], r1[...], r2[...], r3[...]], axis=0)
    out_ref[...] = (dot(rows, w_ref[...]) + bias[...]).astype(jnp.bfloat16)


def project_kernel(first, form, value_ref, w_ref, out0, out1):
    size = out0.shape[0]
    result = form(value_ref[first * size : (first + 2) * size, :], w_ref[...]).astype(jnp.bfloat16)
    out0[...] = result[:size]
    out1[...] = result[size:]


def middle_kernel(in_ref, p0, p1, p2, bias, gain, shift, middle_ref, norm_ref):
    middle = total(in_ref, p0, p1, p2) + bias[...]
    middle_ref[...] = middle
    normed, _ = normalized(middle)
    norm_ref[...] = (normed * gain[...] + shift[...]).astype(jnp.bfloat16)


def middle_back_kernel(middle_ref, p0, p1, p2, up_ref, gain, grads_ref, low_ref, sums_ref):
    upstream = up_ref[...].astype(jnp.float32)
    back, for_gain, for_shift = norm_back(middle_ref[...], gain[...], total(p0, p1, p2))
    grads = upstream + back
    grads_ref[...] = grads
    low_ref[...] = grads.astype(jnp.bfloat16)
    sums_ref[0:1] = jnp.sum(upstream, axis=0, keepdims=True)
    sums_ref[1:2] = for_gain
    sums_ref[2:3] = for_shift
    sums_ref[3:4] = jnp.sum(grads, axis=0, keepdims=True)


def attended_grads_kernel(r0, r1, r2, r3, w_ref, out_ref):
    rows = jnp.concatenate([r0[...], r1[...], r2[...], r3[...]], axis=0)
    out_ref[...] = dot_nt(rows, w_ref[...]).astype(jnp.bfloat16)


def layer_kernel(middle_ref, p0, p1, p2, bias, out_ref):
    out_ref[...] = (total(middle_ref, p0, p1, p2) + bias[...]).astype(jnp.bfloat16)


def last_kernel(in_ref, p0, p1, p2, pairs_ref, w_ref, middle_ref, gain, grads_ref, sums_ref, value_ref):
    hd = value_ref.shape[1]
    grads = total(p0, p1, p2) + dot_nt(pairs_ref[...], w_ref[...])
    back, for_gain, for_shift = norm_back(in_ref[...].astype(jnp.float32), gain[...], grads)
    grads_ref[...] = middle_ref[...] + back
    sums_ref[0:1] = for_gain
    sums_ref[1:2] = for_shift
    value_ref[...] = jnp.sum(pairs_ref[:, hd:].astype(jnp.float32), axis=0, keepdims=True)


def weight_kernel(counts, meta, *refs):
    terms, at = [], 0
    for count in counts:
        terms.append((refs[at : at + 8], refs[at + 8 : at + 8 + count]))
        at += 8 + count
    outs, token, scratch = refs[at : -len(counts) - 1], refs[-len(counts) - 1], refs[-len(counts) :]
    token[...] = jnp.zeros_like(token)

    @pl.when((pl.program_id(0) == 0) & (pl.program_id(1) == 0))
    def _():
        for (_, columns), turned in zip(terms, scratch):
            turn(columns, turned)

    start = 0
    for (rows, _), turned in zip(terms, scratch):
        joined = jnp.concatenate([ref[...] for ref in rows], axis=0)
        part = dot(turned[...], joined).astype(jnp.bfloat16)
        stop = start + part.shape[0]
        outs[0][0, start:stop] = part
        start = stop


def turn(refs, scratch):
    at = 0
    for ref in refs:
        scratch[:, at : at + ref.shape[0]] = ref[...].T
        at += ref.shape[0]


def block_width(rows):
    return (rows if isinstance(rows, jax.Array) else rows[0]).shape[1]


def row_blocks(rows, size, tile, column):
    if isinstance(rows, jax.Array):
        return [pl.BlockSpec((size, tile), lambda *ids, j=j: (ids[-1][2 + j], column(*ids))) for j in range(8)]
    return [pl.BlockSpec((size, tile), lambda *ids: (0, column(*ids)))] * 8


def weight_grads(meta, *terms):
    size, dim = terms[0][1][0].shape[0] * len(terms[0][1]) // 8, block_width(terms[0][0])
    parts = lax.axis_size("seq") // 2
    tile = dim // parts
    column = lambda m, s, meta: 2 * m + s
    specs, args, widths = [], [], []
    for rows, columns in terms:
        specs += row_blocks(rows, size, tile, column)
        specs += [pl.BlockSpec(value.shape, lambda m, s, meta: (0, 0)) for value in columns]
        args += [*([rows] * 8 if isinstance(rows, jax.Array) else rows), *columns]
        widths.append(columns[0].shape[1])
    out = (1, sum(widths), tile)
    out_specs = [
        pl.BlockSpec(out, lambda m, s, meta: (2 * m + s, 0, 0)),
        pl.BlockSpec((8, 128), lambda m, s, meta: (0, 0)),
    ]
    outs = [struct((parts, *out[1:]), jnp.bfloat16), struct((8, 128), jnp.float32)]
    return pl.pallas_call(
        functools.partial(weight_kernel, [len(columns) for _, columns in terms]),
        grid_spec=pltpu.PrefetchScalarGridSpec(
            num_scalar_prefetch=1,
            grid=(parts // 2, 2),
            in_specs=specs,
            out_specs=out_specs,
            scratch_shapes=[pltpu.VMEM((width, 8 * size), jnp.bfloat16) for width in widths],
        ),
        out_shape=outs,
        compiler_params=pltpu.CompilerParams(vmem_limit_bytes=VMEM_LIMIT),
        cost_estimate=LIGHT,
    )(meta, *args)


def slab_kernel(meta, *refs):
    *columns, out_ref, scratch = refs[8:]
    turn(columns, scratch)
    rows = jnp.concatenate([ref[...] for ref in refs[:8]], axis=0)
    out_ref[...] = dot(scratch[...], rows).astype(jnp.bfloat16)


def slab_grads(meta, rows, columns, parts):
    size = columns[0].shape[0] * len(columns) // 8
    tile = block_width(rows) // parts
    width = columns[0].shape[1]
    return pl.pallas_call(
        slab_kernel,
        grid_spec=pltpu.PrefetchScalarGridSpec(
            num_scalar_prefetch=1,
            grid=(1,),
            in_specs=row_blocks(rows, size, tile, lambda m, meta: meta[1])
            + [pl.BlockSpec(value.shape, lambda m, meta: (0, 0)) for value in columns],
            out_specs=pl.BlockSpec((width, tile), lambda m, meta: (0, 0)),
            scratch_shapes=[pltpu.VMEM((width, 8 * size), jnp.bfloat16)],
        ),
        out_shape=struct((width, tile), jnp.bfloat16),
        compiler_params=pltpu.CompilerParams(vmem_limit_bytes=VMEM_LIMIT),
        cost_estimate=LIGHT,
    )(meta, *([rows] * 8 if isinstance(rows, jax.Array) else rows), *columns)


def mlp_kernel(tiles, meta, x0, x1, g0, g1, fc_ref, proj_ref, bias_ref, *refs):
    a_send, a_keep, l_send, l_keep, m0, m1, t0, t1, sum_ref, x_ref, g_ref, macc, tacc = refs
    step = pl.program_id(0)
    size = x0.shape[0]

    @pl.when(step == 0)
    def _():
        x_ref[:size] = x0[...]
        x_ref[size:] = x1[...]
        g_ref[:size] = g0[...]
        g_ref[size:] = g1[...]

    values = dot(x_ref[...], fc_ref[...]) + bias_ref[...]
    grads = dot_nt(g_ref[...], proj_ref[...])
    root = math.sqrt(2 / math.pi)
    square = values * values
    bend = jnp.tanh(root * values * (1 + 0.044715 * square))
    half = 0.5 * (1 + bend)
    slope = half + 0.5 * root * values * (1 - bend * bend) * (1 + 3 * 0.044715 * square)
    activated = (values * half).astype(jnp.bfloat16)
    grads = grads * slope
    sum_ref[...] = jnp.sum(grads, axis=0, keepdims=True)
    low = grads.astype(jnp.bfloat16)

    @pl.when(step == 0)
    def _():
        macc[...] = jnp.zeros_like(macc)
        tacc[...] = jnp.zeros_like(tacc)

    chunk = macc.shape[1] // 4
    for c in range(4):
        cut = slice(c * chunk, (c + 1) * chunk)
        macc[:, cut] += dot(activated, proj_ref[:, cut])
        tacc[:, cut] += dot_nt(low, fc_ref[cut, :])

    @pl.when(step < tiles // 2)
    def _():
        a_send[...] = activated
        l_send[...] = low

    @pl.when(step >= tiles // 2)
    def _():
        a_keep[...] = activated
        l_keep[...] = low

    @pl.when(step == tiles - 1)
    def _():
        f = macc[...].astype(jnp.bfloat16)
        b = tacc[...].astype(jnp.bfloat16)
        m0[...] = f[:size]
        m1[...] = f[size:]
        t0[...] = b[:size]
        t1[...] = b[size:]


def mlp(blocks, ups, meta, w_fc, w_proj, b_fc):
    size, dim = blocks[0].shape
    hidden = w_fc.shape[1]
    tiles = 4
    width = hidden // tiles
    tile = lambda n, meta: ((n // (tiles // 2)) ^ (1 - meta[10])) * (tiles // 2) + n % (tiles // 2)
    fixed = pl.BlockSpec((size, dim), lambda n, meta: (0, 0))
    columns = lambda start: pl.BlockSpec(
        (2 * size, width), lambda n, meta: (0, jnp.clip(n - start, 0, tiles // 2 - 1))
    )
    half = struct((2 * size, hidden // 2), jnp.bfloat16)
    rows = struct((size, dim), jnp.bfloat16)
    return pl.pallas_call(
        functools.partial(mlp_kernel, tiles),
        grid_spec=pltpu.PrefetchScalarGridSpec(
            num_scalar_prefetch=1,
            grid=(tiles,),
            in_specs=[fixed] * 4
            + [
                pl.BlockSpec((dim, width), lambda n, meta: (0, tile(n, meta))),
                pl.BlockSpec((width, dim), lambda n, meta: (tile(n, meta), 0)),
                pl.BlockSpec((1, width), lambda n, meta: (0, tile(n, meta))),
            ],
            out_specs=[columns(0), columns(tiles // 2)] * 2
            + [fixed] * 4
            + [pl.BlockSpec((1, width), lambda n, meta: (0, tile(n, meta)))],
            scratch_shapes=[pltpu.VMEM((2 * size, dim), jnp.bfloat16)] * 2 + [pltpu.VMEM((2 * size, dim), jnp.float32)] * 2,
        ),
        out_shape=[half] * 4 + [rows] * 4 + [struct((1, hidden), jnp.float32)],
        compiler_params=pltpu.CompilerParams(vmem_limit_bytes=VMEM_LIMIT),
        cost_estimate=LIGHT,
    )(meta, *blocks, *ups, w_fc, w_proj, b_fc[None, :])


def allowed_pairs(slot, masks_ref, rows_ref, keys_ref):
    place = keys_ref[...] + masks_ref[2, slot]
    return (place <= rows_ref[0:1, :]) & (place >= rows_ref[1:2, :])


def when_live(meta, slot, visit):
    @pl.when((meta[0, slot] == 1) & (meta[1, slot] == 0))
    def _():
        visit(True)

    @pl.when((meta[0, slot] == 1) & (meta[1, slot] == 1))
    def _():
        visit(False)


def forward_kernel(heads, meta, q_ref, *refs):
    key_refs, value_refs = refs[:4], refs[4:8]
    rows_ref, keys_ref, out_ref, norm_ref, m_ref, l_ref, acc_ref = refs[8:]
    hd = q_ref.shape[1] // heads
    scale = hd ** (-0.5) * LOG2E
    slots = key_refs[0].shape[0]

    def visit(slot, masked, exact):
        keys = jnp.concatenate([ref[slot] for ref in key_refs], axis=0)
        values_t = jnp.concatenate([ref[slot] for ref in value_refs], axis=0).T
        if masked:
            allowed = allowed_pairs(slot, meta, rows_ref, keys_ref)
        def head(h, carry):
            row = pl.ds(h, 1)
            scores = dot_nt(keys, q_ref[:, pl.ds(pl.multiple_of(h * hd, hd), hd)]) * scale
            if masked:
                scores = jnp.where(allowed, scores, NEG)
            top = m_ref[row, :]
            if exact:
                new = jnp.maximum(top, jnp.max(scores, axis=0, keepdims=True))
                decay = jnp.exp2(top - new)
                m_ref[row, :] = new
                l_ref[row, :] = l_ref[row, :] * decay
                acc_ref[h] = acc_ref[h] * decay
                top = new
            weights = jnp.exp2(scores - top)
            l_ref[row, :] += jnp.sum(weights, axis=0, keepdims=True)
            acc_ref[h] += dot(values_t, weights.astype(jnp.bfloat16))
            return carry

        if masked or exact:
            lax.fori_loop(0, heads, head, 0)
        else:
            for h in range(heads):
                head(h, 0)

    def run(exact):
        m_ref[...] = jnp.full_like(m_ref, NEG)
        l_ref[...] = jnp.zeros_like(l_ref)
        acc_ref[...] = jnp.zeros_like(acc_ref)
        visit(0, True, True)

        def body(slot, carry):
            when_live(meta, slot, lambda masked: visit(slot, masked, exact))
            return carry

        lax.fori_loop(1, slots, body, 0)

    run(False)

    @pl.when(jnp.logical_not(jnp.max(l_ref[...]) < 2.0**100))
    def _():
        run(True)

    norm_ref[...] = m_ref[...] + jnp.log2(l_ref[...])
    for h in range(heads):
        result = acc_ref[h] / l_ref[h : h + 1, :]
        out_ref[:, h * hd : (h + 1) * hd] = result.T.astype(jnp.bfloat16)


def backward_visit(heads, slot, meta, q_ref, key_refs, value_refs, rows_ref, keys_ref, norm_ref, up_ref, delta_ref, dq_acc, d_refs):
    hd = q_ref.shape[1] // heads
    part = key_refs[0].shape[1]
    scale = hd ** (-0.5)

    def visit(masked):
        keys = jnp.concatenate([ref[0] for ref in key_refs], axis=0)
        values = jnp.concatenate([ref[0] for ref in value_refs], axis=0)
        keys_t = keys.T
        if masked:
            allowed = allowed_pairs(slot, meta, rows_ref, keys_ref)
        dk = dv = None
        for h in range(heads):
            q = q_ref[:, h * hd : (h + 1) * hd]
            up = up_ref[:, h * hd : (h + 1) * hd]
            weights = jnp.exp2(dot_nt(keys, q) * (scale * LOG2E) - norm_ref[h : h + 1, :])
            if masked:
                weights = jnp.where(allowed, weights, 0.0)
            grads = dot_nt(values, up)
            score_grads = (weights * (grads - delta_ref[h : h + 1, :])).astype(jnp.bfloat16)
            dv_h = dot(weights.astype(jnp.bfloat16), up)
            dk_h = dot(score_grads, q)
            dv = dv_h if dv is None else dv + dv_h
            dk = dk_h if dk is None else dk + dk_h
            dq_acc[h] = dq_acc[h] + dot(keys_t, score_grads)
        for index, ref in enumerate(d_refs):
            part_rows = slice(index * part, (index + 1) * part)
            ref[0, :, :hd] = (dk[part_rows] * scale).astype(jnp.bfloat16)
            ref[0, :, hd:] = dv[part_rows].astype(jnp.bfloat16)

    @pl.when(meta[0, slot] == 0)
    def _():
        for ref in d_refs:
            ref[...] = jnp.zeros_like(ref)

    when_live(meta, slot, visit)


def backward_first_kernel(heads, first, meta, q_ref, *refs):
    key_refs, value_refs = refs[:4], refs[4:8]
    rows_ref, keys_ref, norm_ref, up_ref, att_ref, acc_ref, delta_ref = refs[8:15]
    d_refs = refs[15:19]
    hd = q_ref.shape[1] // heads

    @pl.when(pl.program_id(0) == 0)
    def _():
        acc_ref[...] = jnp.zeros_like(acc_ref)
        for h in range(heads):
            cols = slice(h * hd, (h + 1) * hd)
            both = att_ref[:, cols].astype(jnp.float32) * up_ref[:, cols].astype(jnp.float32)
            delta_ref[h : h + 1, :] = jnp.sum(both.T, axis=0, keepdims=True)

    slot = pl.program_id(0) + first
    backward_visit(heads, slot, meta, q_ref, key_refs, value_refs, rows_ref, keys_ref, norm_ref, up_ref, delta_ref, acc_ref, d_refs)


def backward_last_kernel(heads, first, meta, q_ref, *refs):
    key_refs, value_refs = refs[:4], refs[4:8]
    rows_ref, keys_ref, norm_ref, up_ref, start_ref, delta_ref, dq_ref, bias_ref = refs[8:16]
    d_refs = refs[16:20]
    acc_ref = refs[20]
    hd = q_ref.shape[1] // heads

    @pl.when(pl.program_id(0) == 0)
    def _():
        acc_ref[...] = start_ref[...]

    slot = pl.program_id(0) + first
    backward_visit(heads, slot, meta, q_ref, key_refs, value_refs, rows_ref, keys_ref, norm_ref, up_ref, delta_ref, acc_ref, d_refs)

    @pl.when(pl.program_id(0) == pl.num_programs(0) - 1)
    def _():
        for h in range(heads):
            result = (acc_ref[h] * hd ** (-0.5)).T
            bias_ref[:, h * hd : (h + 1) * hd] = jnp.sum(result, axis=0, keepdims=True)
            dq_ref[:, h * hd : (h + 1) * hd] = result.astype(jnp.bfloat16)


def whole(value):
    return pl.BlockSpec(value.shape, lambda step, meta: (0,) * len(value.shape))


def attention_call(kernel, meta, first, steps, slots, queries, keys, values, extra, outs, scratch, passes):
    rows, width = queries.shape
    part, hd = keys[0].shape[1:]
    block = lambda columns, start: pl.BlockSpec((slots // steps, part, columns), lambda step, meta: (step + start, 0, 0))
    heads = width // hd
    return pl.pallas_call(
        kernel,
        grid_spec=pltpu.PrefetchScalarGridSpec(
            num_scalar_prefetch=1,
            grid=(steps,),
            in_specs=[whole(queries)] + [block(hd, first)] * 8 + [whole(value) for value in extra],
            out_specs=[block(2 * hd, 0) if out.shape == (slots, part, 2 * hd) else whole(out) for out in outs],
            scratch_shapes=scratch,
        ),
        out_shape=outs,
        compiler_params=pltpu.CompilerParams(vmem_limit_bytes=VMEM_LIMIT),
        cost_estimate=LIGHT,
    )(meta, queries, *keys, *values, *extra)


def attention_forward(queries, keys, values, meta, rows_info, keys_info, heads):
    rows, width = queries.shape
    return attention_call(
        functools.partial(forward_kernel, heads), meta, 0, 1, keys[0].shape[0], queries, keys, values,
        [rows_info, keys_info],
        [struct((rows, width), jnp.bfloat16), struct((heads, rows), jnp.float32)],
        [
            pltpu.VMEM((heads, rows), jnp.float32),
            pltpu.VMEM((heads, rows), jnp.float32),
            pltpu.VMEM((heads, width // heads, rows), jnp.float32),
        ],
        2,
    )


def backward_calls(queries, keys, values, meta, rows_info, keys_info, norm, attended, upstream, heads):
    rows, width = queries.shape
    hd = width // heads
    n, part = keys[0].shape[:2]
    half = n // 2
    grads = [struct((half, part, 2 * hd), jnp.bfloat16)] * 4
    shared = [rows_info, keys_info, norm, upstream]

    def first(*deps):
        return attention_call(
            functools.partial(backward_first_kernel, heads, half), meta, half, half, half, tie(queries, *deps),
            keys, values, shared + [attended],
            [struct((heads, hd, rows), jnp.float32), struct((heads, rows), jnp.float32)] + grads,
            [], 5,
        )

    def last(start, delta, *deps):
        return attention_call(
            functools.partial(backward_last_kernel, heads, 0), meta, 0, half, half, tie(queries, *deps),
            keys, values, shared + [start, delta],
            [struct((rows, width), jnp.bfloat16), struct((1, width), jnp.float32)] + grads,
            [pltpu.VMEM((heads, hd, rows), jnp.float32)], 5,
        )

    return first, last


def gather_slots(own, bits, axis):
    found = {0: own}
    for bit in bits:
        masks = sorted(found)
        stacked = jnp.stack([found[m] for m in masks])
        got = swap(stacked, axis, bit)
        found.update({m ^ bit: got[j] for j, m in enumerate(masks)})
    return found


def body(
    hidden_in, lengths, ln1_gain, ln1_bias, w_query, b_query, w_kv, b_value, w_out, b_out,
    ln2_gain, ln2_bias, w_fc, b_fc, w_proj, b_proj, grad_out,
):
    seq_count = lax.axis_size("seq")
    tp_count = lax.axis_size("tp")
    seq_index = lax.axis_index("seq")
    tp_index = lax.axis_index("tp")
    own_rows, dim = hidden_in.shape
    group_rows = own_rows * tp_count
    head_dim = b_value.shape[0]
    heads = w_query.shape[1] // head_dim
    joined = lambda *blocks: jnp.concatenate(blocks, axis=0)
    seq_bits = [1 << j for j in range(seq_count.bit_length() - 1)]

    order = jnp.stack([tp_index, tp_index ^ 1, tp_index ^ 2, tp_index ^ 3]).astype(jnp.int32)
    inside = (order[:, None] * own_rows + jnp.arange(own_rows, dtype=jnp.int32)[None, :]).reshape(-1)
    group_first = seq_index * group_rows
    doc_ends = jnp.cumsum(lengths)
    begins = jnp.max(
        jnp.where(doc_ends[None, :] <= (inside + group_first)[:, None], doc_ends[None, :], 0), axis=1
    )
    rows_info = jnp.stack([inside, begins - group_first])
    keys_info = inside[:, None]
    slot_group = seq_index ^ jnp.arange(seq_count, dtype=jnp.int32)
    key_first = slot_group * group_rows
    live = (slot_group <= seq_index) & (key_first + group_rows > jnp.min(begins))
    clear = (slot_group < seq_index) & (key_first >= jnp.max(begins))
    meta = jnp.stack([live, clear, key_first - group_first]).astype(jnp.int32)
    side = seq_index % 2
    scalar = lambda value: jnp.stack([value]).astype(jnp.int32)
    side_scalar = scalar(side)
    places = [scalar((seq_index // 2) % 2), scalar(2 * tp_index + side)]
    places = jnp.concatenate(places + [side * tp_count + order, (1 - side) * tp_count + order, scalar(side)])
    beside = lambda value: swap(value, "seq", 1)

    row = lambda vector: vector[None, :]
    rows_low = struct((own_rows, dim), jnp.bfloat16)
    rows_wide = struct((own_rows, dim), jnp.float32)
    narrow = struct((own_rows, head_dim), jnp.bfloat16)
    normed_one, key_own, value_own = call(
        first_kernel, [rows_low, narrow, narrow], hidden_in, row(ln1_gain), row(ln1_bias), w_kv, row(b_value)
    )
    key_slots = gather_slots(key_own, seq_bits[::-1], "seq")
    key_stack = jnp.stack([key_slots[m] for m in range(seq_count)])
    value_across = swap(value_own, "tp", 2)
    value_two = jnp.stack([value_own, value_across])
    value_slots = gather_slots(value_two, seq_bits[::-1], "seq")
    value_two = jnp.stack([value_slots[m] for m in range(seq_count)], axis=1)
    value_beside = swap(value_two, "tp", 1)
    values = [value_two[0], value_beside[0], value_two[1], value_beside[1]]
    blocks_one = gather_rows(tie(normed_one, value_across))
    queries = call(
        query_kernel, struct((group_rows, heads * head_dim), jnp.bfloat16), *blocks_one, w_query, row(b_query)
    )
    key_across = tie(swap(key_stack, "tp", 2), queries)
    keys = [key_stack, swap(key_stack, "tp", 1), key_across, swap(key_across, "tp", 1)]
    ups_own = gather_rows(tie(grad_out, queries))
    up_other, one_other = beside(tie(grad_out, queries)), beside(tie(normed_one, queries))
    attended, norm = attention_forward(queries, keys, values, meta, rows_info, keys_info, heads)

    def project(value, weight, form):
        far = call(functools.partial(project_kernel, 2, form), [rows_low] * 2, value, weight)
        near = call(functools.partial(project_kernel, 0, form), [rows_low] * 2, tie(value, far[0]), weight)
        return (*near, *far)

    def scatter(own, beside, across, opposite, *deps):
        over = add_low(tie(across, *deps), swap(opposite, "tp", 1))
        return own, swap(beside, "tp", 1), over, swap(over, "tp", 2)

    att0, att1, _, att2 = scatter(*project(tie(attended, up_other, one_other, ups_own[2]), w_out, dot))
    middle, normed_two = call(
        middle_kernel, [rows_wide, rows_low], hidden_in, att0, att1, att2, row(b_out), row(ln2_gain), row(ln2_bias)
    )

    two_beside, two_across = swap(normed_two, "tp", 1), swap(normed_two, "tp", 2)
    two_other = beside(normed_two)
    act_send0, act_keep0, low_send0, low_keep0, mlp0, mlp1, two0, two1, sum_near = mlp(
        (normed_two, two_beside), ups_own[:2], places, w_fc, w_proj, b_fc
    )
    two_across = tie(two_across, two0)
    two_opposite = swap(two_across, "tp", 1)
    ups_other = half_gather(tie(up_other, two0))
    act_other0 = beside(act_send0)
    act_send1, act_keep1, low_send1, low_keep1, mlp2, mlp3, two2, two3, sum_far = mlp(
        (two_across, two_opposite), ups_own[2:], places, w_fc, w_proj, b_fc
    )

    line = list(line_bits())
    line_side = lambda bit: (seq_index // bit) % 2

    def group_sum(parts):
        groups = [list(range(first, seq_count, 2)) for first in range(2)]
        flat = parts.reshape(-1, parts.shape[2])
        return lax.psum_scatter(flat, "seq", scatter_dimension=0, tiled=True, axis_index_groups=groups)

    def step_sum(state, *deps):
        keep, got, bits = state
        if not bits:
            return state
        keep = tie(keep, *deps)
        send, kept = split_add(line_side(bits[0]), keep, got)
        return kept, swap(send, "seq", bits[0]), bits[1:]

    def halves(*parts):
        rows, columns = parts[0].shape
        return pl.pallas_call(
            halves_kernel,
            in_specs=[pl.BlockSpec(memory_space=pltpu.SMEM)] + [pl.BlockSpec((rows, columns))] * len(parts),
            out_shape=[struct((rows, columns // 2), jnp.bfloat16)] * 2,
            compiler_params=pltpu.CompilerParams(vmem_limit_bytes=VMEM_LIMIT),
            cost_estimate=LIGHT,
        )(side_scalar, *parts)

    def exchange(mine, theirs):
        both = [jnp.where(side == 0, mine, theirs), jnp.where(side == 0, theirs, mine)]
        return joined(*both).astype(jnp.float32)

    act_other1 = beside(act_send1)

    clock = [two2]

    def at(value, *arrived):
        return tie(value, clock[0], *arrived)

    def mark(results):
        clock[0] = results[0] if isinstance(results, (list, tuple)) else results
        return results

    core = lambda value: swap(value, "tp", 1)
    chip = lambda value: swap(value, "tp", 2)

    two_over = mark(add_low(at(two2, act_other0, two_other, ups_other[2]), core(two3)))
    two_own, two_got = core(two1), chip(two_over)
    middle_grads, middle_low, sums_two = mark(
        call(
            middle_back_kernel,
            [rows_wide, rows_low, struct((4, dim), jnp.float32)],
            middle, two0, two_own, two_got, grad_out, at(row(ln2_gain)),
        )
    )
    mid_beside, mid_across = core(middle_low), chip(middle_low)
    low_other0, low_other1 = beside(at(low_send0)), beside(at(low_send1))
    ups = ups_own + full_gather(ups_other, middle_low)
    part_p, clock[0] = weight_grads(places, (ups, (at(act_keep0), act_keep1, act_other0, act_other1)))
    mid_opposite = core(at(mid_across))
    mids_own = (middle_low, mid_beside, mid_across, mid_opposite)

    attended_grads = mark(
        call(attended_grads_kernel, struct(attended.shape, jnp.bfloat16), *mids_own, at(w_out))
    )
    sum_p = group_sum(touch(part_p, mid_across))
    twos_other = half_gather(at(two_other))
    ones_other = half_gather(at(one_other))
    first_call, last_call = backward_calls(
        queries, keys, values, meta, rows_info, keys_info, norm, attended, attended_grads, heads
    )
    start, delta, *kv_far = mark(first_call(attended_grads))
    mid_other = beside(at(middle_low))
    far_over = mark(add_low(at(kv_far[2], low_other0, low_other1, twos_other[2]), core(kv_far[3])))
    twos = (normed_two, two_beside, two_across, two_opposite) + full_gather(twos_other, far_over)
    far_own, far_got = core(kv_far[1]), chip(far_over)
    query_low, bias_query, *kv_near = mark(last_call(start, delta, far_over))

    one2, one3 = mark(
        call(
            functools.partial(project_kernel, 2, dot_nt), [rows_low] * 2,
            at(query_low, far_got, far_own, mid_other, ones_other[2]), w_query,
        )
    )
    ones = blocks_one + full_gather(ones_other, one2)
    near_over = mark(add_low(at(kv_near[2]), core(kv_near[3])))
    mid_others = mid_other, core(at(mid_other)), chip(at(mid_other))
    near_own, near_got = core(kv_near[1]), chip(near_over)
    far_sum = mark(add_low(at(kv_far[0]), far_own, far_got))
    far_there = swap(far_sum, "seq", seq_count // 2)
    one_over = mark(add_low(at(one2), core(one3)))
    one_got = chip(one_over)
    part = struct((group_rows, heads * head_dim // 2), jnp.bfloat16)
    dq_keep, att_keep, sends = mark(
        pl.pallas_call(
            columns_kernel,
            in_specs=[pl.BlockSpec(memory_space=pltpu.SMEM)] + [pl.BlockSpec(query_low.shape)] * 2,
            out_shape=[part, part, struct(query_low.shape, jnp.bfloat16)],
            compiler_params=pltpu.CompilerParams(vmem_limit_bytes=VMEM_LIMIT),
            cost_estimate=LIGHT,
        )(side_scalar, at(query_low), attended)
    )
    others = beside(sends)
    part_f, clock[0] = weight_grads(places, (twos, (at(low_keep0), low_keep1, low_other0, low_other1)))
    kv_slots, there = mark(add_split(at(kv_near[0], others, mid_others[2]), near_own, near_got, far_there))
    sum_f = group_sum(touch(part_f, far_there))
    there = swap(there, "seq", seq_bits[-2])
    mid_others = (*mid_others, core(at(mid_others[2])))
    one0, one1 = mark(
        call(functools.partial(project_kernel, 0, dot_nt), [rows_low] * 2, at(query_low), w_query)
    )
    one_own = core(one1)
    width = dq_keep.shape[1]
    part_qo, clock[0] = weight_grads(
        places,
        (ones, (at(dq_keep), others[:, :width])),
        (mids_own + mid_others, (att_keep, others[:, width:])),
    )
    for bit in seq_bits[-3::-1]:
        kv_slots, send = mark(add_split(at(kv_slots), there))
        there = swap(send, "seq", bit)
    kv_low = mark(add_low(at(kv_slots, one_got), there))[0]
    kv_beside, kv_across = core(kv_low), chip(kv_low)
    sum_qo = group_sum(touch(part_qo, kv_low))
    grad_in, sums_one, sums_value = mark(
        call(
            last_kernel,
            [rows_wide, struct((2, dim), jnp.float32), struct((1, head_dim), jnp.float32)],
            hidden_in, one0, one_own, one_got, kv_low, w_kv, middle_grads, at(row(ln1_gain)),
        )
    )

    count = 6 * dim + head_dim
    vectors = [sums_two.reshape(-1), sums_one.reshape(-1), sums_value[0], bias_query[0], (sum_near + sum_far)[0]]
    vectors = jnp.concatenate(vectors).reshape(-1, 128)
    got = swap(vectors, "seq", seq_bits[1])
    kv_group = joined(kv_low, kv_beside, kv_across, core(at(kv_across)))
    kv_other = beside(kv_group)
    mine_p, theirs_p = mark(halves(at(sum_p)))
    theirs_p = beside(theirs_p)
    mlp_over = mark(add_low(at(mlp2), core(at(mlp3))))
    mlp_own, mlp_got = core(at(mlp1)), chip(mlp_over)
    vectors = vectors + at(got)
    got = swap(vectors, "seq", seq_bits[2])
    part_kv = mark(slab_grads(places, ones, (at(kv_group), kv_other), 2 * tp_count))
    got_kv = swap(part_kv, "seq", seq_bits[1])
    vectors = vectors + at(got)
    for bit in seq_bits[2:]:
        part_kv = mark(add_low(at(part_kv), got_kv))
        got_kv = swap(part_kv, "seq", bit)
    for bit in seq_bits[3:]:
        vectors = vectors + swap(vectors, "seq", bit)
    got = swap(vectors, "seq", 1)
    part_kv = mark(add_low(at(part_kv), got_kv))
    got_kv = beside(part_kv)
    layer_out = mark(call(layer_kernel, rows_low, at(middle), mlp0, mlp_own, mlp_got, row(b_proj)))
    vectors = (vectors + at(got)).reshape(-1)
    shared, split = vectors[:count].reshape(-1, 128), vectors[count:]
    got = chip(shared)
    grad_proj = exchange(at(mine_p), theirs_p)
    half_kv = jnp.where(side == 0, jnp.stack([part_kv, got_kv]), jnp.stack([got_kv, part_kv]))
    half_beside, half_across = core(half_kv), chip(half_kv)
    mine_f, theirs_f = mark(halves(tie(sum_f, half_kv)))
    theirs_f = beside(theirs_f)
    shared = shared + at(got)
    got = core(shared)
    half_opposite = core(at(half_across))
    shared = (shared + at(got)).reshape(-1)
    grad_fc = exchange(at(mine_f), theirs_f).T
    quarters = half_kv, half_beside, half_across, half_opposite
    grad_kv = jnp.concatenate(
        [
            jnp.where(tp_index == j, quarters[0], jnp.where(tp_index == j ^ 1, quarters[1], jnp.where(tp_index == j ^ 2, quarters[2], quarters[3])))
            for j in range(tp_count)
        ]
    )
    grad_kv = jnp.swapaxes(grad_kv.astype(jnp.float32), 1, 2).reshape(dim, 2 * head_dim)
    mine_qo, theirs_qo = mark(halves(tie(sum_qo, grad_fc, grad_kv, shared)))
    theirs_qo = beside(theirs_qo)
    grad_query = exchange(mine_qo[:width], theirs_qo[:width]).T
    grad_out_weight = exchange(mine_qo[width:], theirs_qo[width:])
    queries_width = bias_query.shape[1]
    return (
        layer_out,
        grad_in,
        shared[4 * dim : 5 * dim],
        shared[5 * dim : 6 * dim],
        grad_query,
        split[:queries_width],
        grad_kv,
        shared[6 * dim :],
        grad_out_weight,
        shared[3 * dim : 4 * dim],
        shared[dim : 2 * dim],
        shared[2 * dim : 3 * dim],
        grad_fc,
        split[queries_width:],
        grad_proj,
        shared[:dim],
    )


def solution(mesh):
    placed = (
        P(("seq", "tp"), None), P(), P(), P(), P(None, "tp"), P("tp"), P(), P(), P("tp", None),
        P(), P(), P(), P(None, "tp"), P("tp"), P("tp", None), P(), P(("seq", "tp"), None),
    )
    returned = (
        P(("seq", "tp"), None), P(("seq", "tp"), None), P(), P(), P("seq", "tp"), P("tp"), P(), P(),
        P("tp", "seq"), P(), P(), P(), P("seq", "tp"), P("tp"), P("tp", "seq"), P(),
    )
    return jax.shard_map(body, mesh=mesh, in_specs=placed, out_specs=returned, check_vma=False)
```

```python
import functools
import math

import jax
import jax.numpy as jnp
from jax import lax
from jax.experimental import pallas as pl
from jax.experimental.pallas import tpu as pltpu
from jax.sharding import PartitionSpec as P

EPS = 1e-05
NEG = -1e30
LOG2E = math.log2(math.e)
VMEM_LIMIT = 60 * 1024 * 1024
LIGHT = pl.CostEstimate(flops=1024, bytes_accessed=1024, transcendentals=0)
NT = (((1,), (1,)), ((), ()))


def dot(left, right):
    return jnp.dot(left, right, preferred_element_type=jnp.float32)


def dot_nt(left, right):
    return lax.dot_general(left, right, NT, preferred_element_type=jnp.float32)


def tie(value, *deps):
    return lax.optimization_barrier((value, *deps))[0]


def struct(shape, dtype):
    return jax.ShapeDtypeStruct(shape, dtype)


def swap(value, axis, bit):
    count = lax.axis_size(axis)
    return lax.ppermute(value, axis, [(j, j ^ bit) for j in range(count)])


def gather_rows(own):
    beside = swap(own, "tp", 1)
    across = swap(own, "tp", 2)
    return own, beside, across, swap(across, "tp", 1)


def touch_kernel(value, out):
    pass


def touch(value, *deps):
    anywhere = pl.BlockSpec(memory_space=pl.ANY)
    return pl.pallas_call(
        touch_kernel,
        in_specs=[anywhere],
        out_specs=anywhere,
        out_shape=struct(value.shape, value.dtype),
        input_output_aliases={0: 0},
        cost_estimate=LIGHT,
    )(tie(value, *deps))


def gather_pair(own):
    seq_count, tp_count = lax.axis_size("seq"), lax.axis_size("tp")
    wide = 2 * tp_count
    groups = [[first * wide + j for j in range(wide)] for first in range(seq_count // 2)]
    return lax.all_gather(own, ("seq", "tp"), axis=0, tiled=True, axis_index_groups=groups)


def half_gather(own):
    return own, swap(own, "tp", 1), swap(own, "tp", 2)


def full_gather(blocks, after):
    own, beside, across = blocks
    across = tie(across, after)
    return own, beside, across, swap(across, "tp", 1)


def call(kernel, outs, *args):
    return pl.pallas_call(
        kernel,
        out_shape=outs,
        compiler_params=pltpu.CompilerParams(vmem_limit_bytes=VMEM_LIMIT),
        cost_estimate=LIGHT,
    )(*args)


def total(*refs):
    return sum(ref[...].astype(jnp.float32) for ref in refs)


def add_kernel(*refs):
    refs[-1][...] = total(*refs[:-1]).astype(jnp.bfloat16)


def add_split_kernel(*refs):
    *parts, low_ref, high_ref = refs
    both = total(*parts).astype(jnp.bfloat16)
    half = low_ref.shape[0]
    low_ref[...] = both[:half]
    high_ref[...] = both[half:]


def add_split(*values):
    half = struct((values[0].shape[0] // 2, *values[0].shape[1:]), jnp.bfloat16)
    return call(add_split_kernel, [half, half], *values)


def columns_kernel(side, first, second, first_keep, second_keep, send):
    half = first_keep.shape[1]
    for index, (ref, keep) in enumerate(((first, first_keep), (second, second_keep))):
        low, high = ref[:, :half], ref[:, half:]
        keep[...] = jnp.where(side[0] == 0, low, high)
        send[:, index * half : (index + 1) * half] = jnp.where(side[0] == 0, high, low)


def add_low(*values):
    return call(add_kernel, struct(values[0].shape, jnp.bfloat16), *values)


def split_kernel(meta, keep_in, got_in, send_ref, keep_ref):
    both = total(keep_in, got_in).astype(jnp.bfloat16)

    @pl.when(pl.program_id(1) == 0)
    def _():
        send_ref[...] = both

    @pl.when(pl.program_id(1) == 1)
    def _():
        keep_ref[...] = both


def halves_kernel(side, *refs):
    *parts, mine, theirs = refs
    half = mine.shape[1]
    both = total(*parts).astype(jnp.bfloat16)
    low, high = both[:, :half], both[:, half:]
    mine[...] = jnp.where(side[0] == 0, low, high)
    theirs[...] = jnp.where(side[0] == 0, high, low)


def split_add(side, keep, got):
    parts, rows, columns = keep.shape
    block = pl.BlockSpec((1, rows, columns), lambda m, s, meta: (2 * m + (meta[0] + 1 - s) % 2, 0, 0))
    half = struct((parts // 2, rows, columns), jnp.bfloat16)
    return pl.pallas_call(
        split_kernel,
        grid_spec=pltpu.PrefetchScalarGridSpec(
            num_scalar_prefetch=1,
            grid=(parts // 2, 2),
            in_specs=[block, block],
            out_specs=[pl.BlockSpec((1, rows, columns), lambda m, s, meta: (m, 0, 0))] * 2,
        ),
        out_shape=[half, half],
        compiler_params=pltpu.CompilerParams(vmem_limit_bytes=VMEM_LIMIT),
        cost_estimate=LIGHT,
    )(jnp.stack([side]).astype(jnp.int32), keep, got)


def line_bits():
    bit = 2
    while bit < lax.axis_size("seq"):
        yield bit
        bit *= 2


def column_halves(value):
    side = lax.axis_index("seq") % 2
    half = value.shape[1] // 2
    keep = lax.dynamic_slice_in_dim(value, side * half, half, 1)
    send = lax.dynamic_slice_in_dim(value, (1 - side) * half, half, 1)
    return keep, send


def sum_over(value, axis):
    bit = 1
    while bit < lax.axis_size(axis):
        value = value + swap(value, axis, bit)
        bit *= 2
    return value


def normalized(features):
    centered = features - jnp.mean(features, axis=-1, keepdims=True)
    variance = jnp.mean(centered * centered, axis=-1, keepdims=True)
    scale = lax.rsqrt(variance + EPS)
    return centered * scale, scale


def norm_back(features, gain, grads):
    normed, scale = normalized(features)
    scaled = grads * gain
    mean = jnp.mean(scaled, axis=-1, keepdims=True)
    along = jnp.mean(scaled * normed, axis=-1, keepdims=True)
    over_rows = lambda value: jnp.sum(value, axis=0, keepdims=True)
    return scale * (scaled - mean - normed * along), over_rows(grads * normed), over_rows(grads)


def first_kernel(in_ref, gain, shift, w_ref, bias, norm_ref, key_ref, value_ref):
    normed, _ = normalized(in_ref[...].astype(jnp.float32))
    low = (normed * gain[...] + shift[...]).astype(jnp.bfloat16)
    norm_ref[...] = low
    pairs = dot(low, w_ref[...])
    hd = key_ref.shape[1]
    key_ref[...] = pairs[:, :hd].astype(jnp.bfloat16)
    value_ref[...] = (pairs[:, hd:] + bias[...]).astype(jnp.bfloat16)


def query_kernel(r0, r1, r2, r3, w_ref, bias, out_ref):
    rows = jnp.concatenate([r0[...], r1[...], r2[...], r3[...]], axis=0)
    out_ref[...] = (dot(rows, w_ref[...]) + bias[...]).astype(jnp.bfloat16)


def project_kernel(first, form, value_ref, w_ref, out0, out1):
    size = out0.shape[0]
    result = form(value_ref[first * size : (first + 2) * size, :], w_ref[...]).astype(jnp.bfloat16)
    out0[...] = result[:size]
    out1[...] = result[size:]


def middle_kernel(in_ref, p0, p1, p2, bias, gain, shift, middle_ref, norm_ref):
    middle = total(in_ref, p0, p1, p2) + bias[...]
    middle_ref[...] = middle
    normed, _ = normalized(middle)
    norm_ref[...] = (normed * gain[...] + shift[...]).astype(jnp.bfloat16)


def middle_back_kernel(middle_ref, p0, p1, p2, up_ref, gain, grads_ref, low_ref, sums_ref):
    upstream = up_ref[...].astype(jnp.float32)
    back, for_gain, for_shift = norm_back(middle_ref[...], gain[...], total(p0, p1, p2))
    grads = upstream + back
    grads_ref[...] = grads
    low_ref[...] = grads.astype(jnp.bfloat16)
    sums_ref[0:1] = jnp.sum(upstream, axis=0, keepdims=True)
    sums_ref[1:2] = for_gain
    sums_ref[2:3] = for_shift
    sums_ref[3:4] = jnp.sum(grads, axis=0, keepdims=True)


def attended_grads_kernel(r0, r1, r2, r3, w_ref, out_ref):
    rows = jnp.concatenate([r0[...], r1[...], r2[...], r3[...]], axis=0)
    out_ref[...] = dot_nt(rows, w_ref[...]).astype(jnp.bfloat16)


def layer_kernel(middle_ref, p0, p1, p2, bias, out_ref):
    out_ref[...] = (total(middle_ref, p0, p1, p2) + bias[...]).astype(jnp.bfloat16)


def last_kernel(in_ref, p0, p1, p2, pairs_ref, w_ref, middle_ref, gain, grads_ref, sums_ref, value_ref):
    hd = value_ref.shape[1]
    grads = total(p0, p1, p2) + dot_nt(pairs_ref[...], w_ref[...])
    back, for_gain, for_shift = norm_back(in_ref[...].astype(jnp.float32), gain[...], grads)
    grads_ref[...] = middle_ref[...] + back
    sums_ref[0:1] = for_gain
    sums_ref[1:2] = for_shift
    value_ref[...] = jnp.sum(pairs_ref[:, hd:].astype(jnp.float32), axis=0, keepdims=True)


def weight_kernel(counts, meta, *refs):
    terms, at = [], 0
    for count in counts:
        terms.append((refs[at : at + 8], refs[at + 8 : at + 8 + count]))
        at += 8 + count
    outs, token, scratch = refs[at : -len(counts) - 1], refs[-len(counts) - 1], refs[-len(counts) :]
    token[...] = jnp.zeros_like(token)

    @pl.when((pl.program_id(0) == 0) & (pl.program_id(1) == 0))
    def _():
        for (_, columns), turned in zip(terms, scratch):
            turn(columns, turned)

    start = 0
    for (rows, _), turned in zip(terms, scratch):
        joined = jnp.concatenate([ref[...] for ref in rows], axis=0)
        part = dot(turned[...], joined).astype(jnp.bfloat16)
        stop = start + part.shape[0]
        outs[0][0, start:stop] = part
        start = stop


def turn(refs, scratch):
    at = 0
    for ref in refs:
        scratch[:, at : at + ref.shape[0]] = ref[...].T
        at += ref.shape[0]


def block_width(rows):
    return (rows if isinstance(rows, jax.Array) else rows[0]).shape[1]


def row_blocks(rows, size, tile, column):
    if isinstance(rows, jax.Array):
        return [pl.BlockSpec((size, tile), lambda *ids, j=j: (ids[-1][2 + j], column(*ids))) for j in range(8)]
    return [pl.BlockSpec((size, tile), lambda *ids: (0, column(*ids)))] * 8


def weight_grads(meta, *terms):
    size, dim = terms[0][1][0].shape[0] * len(terms[0][1]) // 8, block_width(terms[0][0])
    parts = lax.axis_size("seq") // 2
    tile = dim // parts
    column = lambda m, s, meta: 2 * m + s
    specs, args, widths = [], [], []
    for rows, columns in terms:
        specs += row_blocks(rows, size, tile, column)
        specs += [pl.BlockSpec(value.shape, lambda m, s, meta: (0, 0)) for value in columns]
        args += [*([rows] * 8 if isinstance(rows, jax.Array) else rows), *columns]
        widths.append(columns[0].shape[1])
    out = (1, sum(widths), tile)
    out_specs = [
        pl.BlockSpec(out, lambda m, s, meta: (2 * m + s, 0, 0)),
        pl.BlockSpec((8, 128), lambda m, s, meta: (0, 0)),
    ]
    outs = [struct((parts, *out[1:]), jnp.bfloat16), struct((8, 128), jnp.float32)]
    return pl.pallas_call(
        functools.partial(weight_kernel, [len(columns) for _, columns in terms]),
        grid_spec=pltpu.PrefetchScalarGridSpec(
            num_scalar_prefetch=1,
            grid=(parts // 2, 2),
            in_specs=specs,
            out_specs=out_specs,
            scratch_shapes=[pltpu.VMEM((width, 8 * size), jnp.bfloat16) for width in widths],
        ),
        out_shape=outs,
        compiler_params=pltpu.CompilerParams(vmem_limit_bytes=VMEM_LIMIT),
        cost_estimate=LIGHT,
    )(meta, *args)


def slab_kernel(meta, *refs):
    *columns, out_ref, scratch = refs[8:]
    turn(columns, scratch)
    rows = jnp.concatenate([ref[...] for ref in refs[:8]], axis=0)
    out_ref[...] = dot(scratch[...], rows).astype(jnp.bfloat16)


def slab_grads(meta, rows, columns, parts):
    size = columns[0].shape[0] * len(columns) // 8
    tile = block_width(rows) // parts
    width = columns[0].shape[1]
    return pl.pallas_call(
        slab_kernel,
        grid_spec=pltpu.PrefetchScalarGridSpec(
            num_scalar_prefetch=1,
            grid=(1,),
            in_specs=row_blocks(rows, size, tile, lambda m, meta: meta[1])
            + [pl.BlockSpec(value.shape, lambda m, meta: (0, 0)) for value in columns],
            out_specs=pl.BlockSpec((width, tile), lambda m, meta: (0, 0)),
            scratch_shapes=[pltpu.VMEM((width, 8 * size), jnp.bfloat16)],
        ),
        out_shape=struct((width, tile), jnp.bfloat16),
        compiler_params=pltpu.CompilerParams(vmem_limit_bytes=VMEM_LIMIT),
        cost_estimate=LIGHT,
    )(meta, *([rows] * 8 if isinstance(rows, jax.Array) else rows), *columns)


def mlp_kernel(tiles, meta, x0, x1, g0, g1, fc_ref, proj_ref, bias_ref, *refs):
    a_send, a_keep, l_send, l_keep, m0, m1, t0, t1, sum_ref, x_ref, g_ref, macc, tacc = refs
    step = pl.program_id(0)
    size = x0.shape[0]

    @pl.when(step == 0)
    def _():
        x_ref[:size] = x0[...]
        x_ref[size:] = x1[...]
        g_ref[:size] = g0[...]
        g_ref[size:] = g1[...]

    values = dot(x_ref[...], fc_ref[...]) + bias_ref[...]
    grads = dot_nt(g_ref[...], proj_ref[...])
    root = math.sqrt(2 / math.pi)
    square = values * values
    bend = jnp.tanh(root * values * (1 + 0.044715 * square))
    half = 0.5 * (1 + bend)
    slope = half + 0.5 * root * values * (1 - bend * bend) * (1 + 3 * 0.044715 * square)
    activated = (values * half).astype(jnp.bfloat16)
    grads = grads * slope
    sum_ref[...] = jnp.sum(grads, axis=0, keepdims=True)
    low = grads.astype(jnp.bfloat16)

    @pl.when(step == 0)
    def _():
        macc[...] = jnp.zeros_like(macc)
        tacc[...] = jnp.zeros_like(tacc)

    chunk = macc.shape[1] // 4
    for c in range(4):
        cut = slice(c * chunk, (c + 1) * chunk)
        macc[:, cut] += dot(activated, proj_ref[:, cut])
        tacc[:, cut] += dot_nt(low, fc_ref[cut, :])

    @pl.when(step < tiles // 2)
    def _():
        a_send[...] = activated
        l_send[...] = low

    @pl.when(step >= tiles // 2)
    def _():
        a_keep[...] = activated
        l_keep[...] = low

    @pl.when(step == tiles - 1)
    def _():
        f = macc[...].astype(jnp.bfloat16)
        b = tacc[...].astype(jnp.bfloat16)
        m0[...] = f[:size]
        m1[...] = f[size:]
        t0[...] = b[:size]
        t1[...] = b[size:]


def mlp(blocks, ups, meta, w_fc, w_proj, b_fc):
    size, dim = blocks[0].shape
    hidden = w_fc.shape[1]
    tiles = 4
    width = hidden // tiles
    tile = lambda n, meta: ((n // (tiles // 2)) ^ (1 - meta[10])) * (tiles // 2) + n % (tiles // 2)
    fixed = pl.BlockSpec((size, dim), lambda n, meta: (0, 0))
    columns = lambda start: pl.BlockSpec(
        (2 * size, width), lambda n, meta: (0, jnp.clip(n - start, 0, tiles // 2 - 1))
    )
    half = struct((2 * size, hidden // 2), jnp.bfloat16)
    rows = struct((size, dim), jnp.bfloat16)
    return pl.pallas_call(
        functools.partial(mlp_kernel, tiles),
        grid_spec=pltpu.PrefetchScalarGridSpec(
            num_scalar_prefetch=1,
            grid=(tiles,),
            in_specs=[fixed] * 4
            + [
                pl.BlockSpec((dim, width), lambda n, meta: (0, tile(n, meta))),
                pl.BlockSpec((width, dim), lambda n, meta: (tile(n, meta), 0)),
                pl.BlockSpec((1, width), lambda n, meta: (0, tile(n, meta))),
            ],
            out_specs=[columns(0), columns(tiles // 2)] * 2
            + [fixed] * 4
            + [pl.BlockSpec((1, width), lambda n, meta: (0, tile(n, meta)))],
            scratch_shapes=[pltpu.VMEM((2 * size, dim), jnp.bfloat16)] * 2 + [pltpu.VMEM((2 * size, dim), jnp.float32)] * 2,
        ),
        out_shape=[half] * 4 + [rows] * 4 + [struct((1, hidden), jnp.float32)],
        compiler_params=pltpu.CompilerParams(vmem_limit_bytes=VMEM_LIMIT),
        cost_estimate=LIGHT,
    )(meta, *blocks, *ups, w_fc, w_proj, b_fc[None, :])


def allowed_pairs(slot, masks_ref, rows_ref, keys_ref):
    place = keys_ref[...] + masks_ref[2, slot]
    return (place <= rows_ref[0:1, :]) & (place >= rows_ref[1:2, :])


def when_live(meta, slot, visit):
    @pl.when((meta[0, slot] == 1) & (meta[1, slot] == 0))
    def _():
        visit(True)

    @pl.when((meta[0, slot] == 1) & (meta[1, slot] == 1))
    def _():
        visit(False)


def forward_kernel(heads, meta, q_ref, *refs):
    key_refs, value_refs = refs[:4], refs[4:8]
    rows_ref, keys_ref, out_ref, norm_ref, m_ref, l_ref, acc_ref = refs[8:]
    hd = q_ref.shape[1] // heads
    scale = hd ** (-0.5) * LOG2E
    slots = key_refs[0].shape[0]

    def visit(slot, masked, exact):
        keys = jnp.concatenate([ref[slot] for ref in key_refs], axis=0)
        values_t = jnp.concatenate([ref[slot] for ref in value_refs], axis=0).T
        if masked:
            allowed = allowed_pairs(slot, meta, rows_ref, keys_ref)
        for h in range(heads):
            scores = dot_nt(keys, q_ref[:, h * hd : (h + 1) * hd]) * scale
            if masked:
                scores = jnp.where(allowed, scores, NEG)
            top = m_ref[h : h + 1, :]
            if exact:
                new = jnp.maximum(top, jnp.max(scores, axis=0, keepdims=True))
                decay = jnp.exp2(top - new)
                m_ref[h : h + 1, :] = new
                l_ref[h : h + 1, :] = l_ref[h : h + 1, :] * decay
                acc_ref[h] = acc_ref[h] * decay
                top = new
            weights = jnp.exp2(scores - top)
            l_ref[h : h + 1, :] += jnp.sum(weights, axis=0, keepdims=True)
            acc_ref[h] += dot(values_t, weights.astype(jnp.bfloat16))

    def run(exact):
        m_ref[...] = jnp.full_like(m_ref, NEG)
        l_ref[...] = jnp.zeros_like(l_ref)
        acc_ref[...] = jnp.zeros_like(acc_ref)
        visit(0, True, True)

        def body(slot, carry):
            when_live(meta, slot, lambda masked: visit(slot, masked, exact))
            return carry

        lax.fori_loop(1, slots, body, 0)

    run(False)

    @pl.when(jnp.logical_not(jnp.max(l_ref[...]) < 2.0**100))
    def _():
        run(True)

    norm_ref[...] = m_ref[...] + jnp.log2(l_ref[...])
    for h in range(heads):
        result = acc_ref[h] / l_ref[h : h + 1, :]
        out_ref[:, h * hd : (h + 1) * hd] = result.T.astype(jnp.bfloat16)


def backward_visit(heads, slot, meta, q_ref, key_refs, value_refs, rows_ref, keys_ref, norm_ref, up_ref, delta_ref, dq_acc, d_refs):
    hd = q_ref.shape[1] // heads
    part = key_refs[0].shape[1]
    scale = hd ** (-0.5)

    def visit(masked):
        keys = jnp.concatenate([ref[0] for ref in key_refs], axis=0)
        values = jnp.concatenate([ref[0] for ref in value_refs], axis=0)
        keys_t = keys.T
        if masked:
            allowed = allowed_pairs(slot, meta, rows_ref, keys_ref)
        dk = dv = None
        for h in range(heads):
            q = q_ref[:, h * hd : (h + 1) * hd]
            up = up_ref[:, h * hd : (h + 1) * hd]
            weights = jnp.exp2(dot_nt(keys, q) * (scale * LOG2E) - norm_ref[h : h + 1, :])
            if masked:
                weights = jnp.where(allowed, weights, 0.0)
            grads = dot_nt(values, up)
            score_grads = (weights * (grads - delta_ref[h : h + 1, :])).astype(jnp.bfloat16)
            dv_h = dot(weights.astype(jnp.bfloat16), up)
            dk_h = dot(score_grads, q)
            dv = dv_h if dv is None else dv + dv_h
            dk = dk_h if dk is None else dk + dk_h
            dq_acc[h] = dq_acc[h] + dot(keys_t, score_grads)
        for index, ref in enumerate(d_refs):
            part_rows = slice(index * part, (index + 1) * part)
            ref[0, :, :hd] = (dk[part_rows] * scale).astype(jnp.bfloat16)
            ref[0, :, hd:] = dv[part_rows].astype(jnp.bfloat16)

    @pl.when(meta[0, slot] == 0)
    def _():
        for ref in d_refs:
            ref[...] = jnp.zeros_like(ref)

    when_live(meta, slot, visit)


def backward_first_kernel(heads, first, meta, q_ref, *refs):
    key_refs, value_refs = refs[:4], refs[4:8]
    rows_ref, keys_ref, norm_ref, up_ref, att_ref, acc_ref, delta_ref = refs[8:15]
    d_refs = refs[15:19]
    hd = q_ref.shape[1] // heads

    @pl.when(pl.program_id(0) == 0)
    def _():
        acc_ref[...] = jnp.zeros_like(acc_ref)
        for h in range(heads):
            cols = slice(h * hd, (h + 1) * hd)
            both = att_ref[:, cols].astype(jnp.float32) * up_ref[:, cols].astype(jnp.float32)
            delta_ref[h : h + 1, :] = jnp.sum(both.T, axis=0, keepdims=True)

    slot = pl.program_id(0) + first
    backward_visit(heads, slot, meta, q_ref, key_refs, value_refs, rows_ref, keys_ref, norm_ref, up_ref, delta_ref, acc_ref, d_refs)


def backward_last_kernel(heads, first, meta, q_ref, *refs):
    key_refs, value_refs = refs[:4], refs[4:8]
    rows_ref, keys_ref, norm_ref, up_ref, start_ref, delta_ref, dq_ref, bias_ref = refs[8:16]
    d_refs = refs[16:20]
    acc_ref = refs[20]
    hd = q_ref.shape[1] // heads

    @pl.when(pl.program_id(0) == 0)
    def _():
        acc_ref[...] = start_ref[...]

    slot = pl.program_id(0) + first
    backward_visit(heads, slot, meta, q_ref, key_refs, value_refs, rows_ref, keys_ref, norm_ref, up_ref, delta_ref, acc_ref, d_refs)

    @pl.when(pl.program_id(0) == pl.num_programs(0) - 1)
    def _():
        for h in range(heads):
            result = (acc_ref[h] * hd ** (-0.5)).T
            bias_ref[:, h * hd : (h + 1) * hd] = jnp.sum(result, axis=0, keepdims=True)
            dq_ref[:, h * hd : (h + 1) * hd] = result.astype(jnp.bfloat16)


def whole(value):
    return pl.BlockSpec(value.shape, lambda step, meta: (0,) * len(value.shape))


def attention_call(kernel, meta, first, steps, slots, queries, keys, values, extra, outs, scratch, passes):
    rows, width = queries.shape
    part, hd = keys[0].shape[1:]
    block = lambda columns, start: pl.BlockSpec((slots // steps, part, columns), lambda step, meta: (step + start, 0, 0))
    heads = width // hd
    return pl.pallas_call(
        kernel,
        grid_spec=pltpu.PrefetchScalarGridSpec(
            num_scalar_prefetch=1,
            grid=(steps,),
            in_specs=[whole(queries)] + [block(hd, first)] * 8 + [whole(value) for value in extra],
            out_specs=[block(2 * hd, 0) if out.shape == (slots, part, 2 * hd) else whole(out) for out in outs],
            scratch_shapes=scratch,
        ),
        out_shape=outs,
        compiler_params=pltpu.CompilerParams(vmem_limit_bytes=VMEM_LIMIT),
        cost_estimate=LIGHT,
    )(meta, queries, *keys, *values, *extra)


def attention_forward(queries, keys, values, meta, rows_info, keys_info, heads):
    rows, width = queries.shape
    return attention_call(
        functools.partial(forward_kernel, heads), meta, 0, 1, keys[0].shape[0], queries, keys, values,
        [rows_info, keys_info],
        [struct((rows, width), jnp.bfloat16), struct((heads, rows), jnp.float32)],
        [
            pltpu.VMEM((heads, rows), jnp.float32),
            pltpu.VMEM((heads, rows), jnp.float32),
            pltpu.VMEM((heads, width // heads, rows), jnp.float32),
        ],
        2,
    )


def backward_calls(queries, keys, values, meta, rows_info, keys_info, norm, attended, upstream, heads):
    rows, width = queries.shape
    hd = width // heads
    n, part = keys[0].shape[:2]
    half = n // 2
    grads = [struct((half, part, 2 * hd), jnp.bfloat16)] * 4
    shared = [rows_info, keys_info, norm, upstream]

    def first(*deps):
        return attention_call(
            functools.partial(backward_first_kernel, heads, half), meta, half, half, half, tie(queries, *deps),
            keys, values, shared + [attended],
            [struct((heads, hd, rows), jnp.float32), struct((heads, rows), jnp.float32)] + grads,
            [], 5,
        )

    def last(start, delta, *deps):
        return attention_call(
            functools.partial(backward_last_kernel, heads, 0), meta, 0, half, half, tie(queries, *deps),
            keys, values, shared + [start, delta],
            [struct((rows, width), jnp.bfloat16), struct((1, width), jnp.float32)] + grads,
            [pltpu.VMEM((heads, hd, rows), jnp.float32)], 5,
        )

    return first, last


def gather_slots(own, bits, axis):
    found = {0: own}
    for bit in bits:
        masks = sorted(found)
        stacked = jnp.stack([found[m] for m in masks])
        got = swap(stacked, axis, bit)
        found.update({m ^ bit: got[j] for j, m in enumerate(masks)})
    return found


def body(
    hidden_in, lengths, ln1_gain, ln1_bias, w_query, b_query, w_kv, b_value, w_out, b_out,
    ln2_gain, ln2_bias, w_fc, b_fc, w_proj, b_proj, grad_out,
):
    seq_count = lax.axis_size("seq")
    tp_count = lax.axis_size("tp")
    seq_index = lax.axis_index("seq")
    tp_index = lax.axis_index("tp")
    own_rows, dim = hidden_in.shape
    group_rows = own_rows * tp_count
    head_dim = b_value.shape[0]
    heads = w_query.shape[1] // head_dim
    joined = lambda *blocks: jnp.concatenate(blocks, axis=0)
    seq_bits = [1 << j for j in range(seq_count.bit_length() - 1)]

    order = jnp.stack([tp_index, tp_index ^ 1, tp_index ^ 2, tp_index ^ 3]).astype(jnp.int32)
    inside = (order[:, None] * own_rows + jnp.arange(own_rows, dtype=jnp.int32)[None, :]).reshape(-1)
    group_first = seq_index * group_rows
    doc_ends = jnp.cumsum(lengths)
    begins = jnp.max(
        jnp.where(doc_ends[None, :] <= (inside + group_first)[:, None], doc_ends[None, :], 0), axis=1
    )
    rows_info = jnp.stack([inside, begins - group_first])
    keys_info = inside[:, None]
    slot_group = seq_index ^ jnp.arange(seq_count, dtype=jnp.int32)
    key_first = slot_group * group_rows
    live = (slot_group <= seq_index) & (key_first + group_rows > jnp.min(begins))
    clear = (slot_group < seq_index) & (key_first >= jnp.max(begins))
    meta = jnp.stack([live, clear, key_first - group_first]).astype(jnp.int32)
    side = seq_index % 2
    scalar = lambda value: jnp.stack([value]).astype(jnp.int32)
    side_scalar = scalar(side)
    places = [scalar((seq_index // 2) % 2), scalar(2 * tp_index + side)]
    places = jnp.concatenate(places + [side * tp_count + order, (1 - side) * tp_count + order, scalar(side)])
    beside = lambda value: swap(value, "seq", 1)

    row = lambda vector: vector[None, :]
    rows_low = struct((own_rows, dim), jnp.bfloat16)
    rows_wide = struct((own_rows, dim), jnp.float32)
    narrow = struct((own_rows, head_dim), jnp.bfloat16)
    normed_one, key_own, value_own = call(
        first_kernel, [rows_low, narrow, narrow], hidden_in, row(ln1_gain), row(ln1_bias), w_kv, row(b_value)
    )
    key_slots = gather_slots(key_own, seq_bits[::-1], "seq")
    key_stack = jnp.stack([key_slots[m] for m in range(seq_count)])
    value_two = jnp.stack([value_own, swap(value_own, "tp", 2)])
    value_slots = gather_slots(value_two, seq_bits[::-1], "seq")
    value_two = jnp.stack([value_slots[m] for m in range(seq_count)], axis=1)
    value_beside = swap(value_two, "tp", 1)
    values = [value_two[0], value_beside[0], value_two[1], value_beside[1]]
    blocks_one = gather_rows(normed_one)
    queries = call(
        query_kernel, struct((group_rows, heads * head_dim), jnp.bfloat16), *blocks_one, w_query, row(b_query)
    )
    key_across = tie(swap(key_stack, "tp", 2), queries)
    keys = [key_stack, swap(key_stack, "tp", 1), key_across, swap(key_across, "tp", 1)]
    ups_own = gather_rows(tie(grad_out, queries))
    up_other, one_other = beside(tie(grad_out, queries)), beside(tie(normed_one, queries))
    attended, norm = attention_forward(queries, keys, values, meta, rows_info, keys_info, heads)

    def project(value, weight, form):
        far = call(functools.partial(project_kernel, 2, form), [rows_low] * 2, value, weight)
        near = call(functools.partial(project_kernel, 0, form), [rows_low] * 2, tie(value, far[0]), weight)
        return (*near, *far)

    def scatter(own, beside, across, opposite, *deps):
        over = add_low(tie(across, *deps), swap(opposite, "tp", 1))
        return own, swap(beside, "tp", 1), over, swap(over, "tp", 2)

    att0, att1, _, att2 = scatter(*project(attended, w_out, dot))
    middle, normed_two = call(
        middle_kernel, [rows_wide, rows_low], hidden_in, att0, att1, att2, row(b_out), row(ln2_gain), row(ln2_bias)
    )

    two_beside, two_across = swap(normed_two, "tp", 1), swap(normed_two, "tp", 2)
    two_other = beside(normed_two)
    act_send0, act_keep0, low_send0, low_keep0, mlp0, mlp1, two0, two1, sum_near = mlp(
        (normed_two, tie(two_beside, up_other, one_other)), ups_own[:2], places, w_fc, w_proj, b_fc
    )
    two_across = tie(two_across, two0)
    two_opposite = swap(two_across, "tp", 1)
    ups_other = half_gather(tie(up_other, two0))
    act_other0 = beside(act_send0)
    act_send1, act_keep1, low_send1, low_keep1, mlp2, mlp3, two2, two3, sum_far = mlp(
        (two_across, two_opposite), ups_own[2:], places, w_fc, w_proj, b_fc
    )

    line = list(line_bits())
    line_side = lambda bit: (seq_index // bit) % 2

    def group_sum(parts):
        groups = [list(range(first, seq_count, 2)) for first in range(2)]
        flat = parts.reshape(-1, parts.shape[2])
        return lax.psum_scatter(flat, "seq", scatter_dimension=0, tiled=True, axis_index_groups=groups)

    def step_sum(state, *deps):
        keep, got, bits = state
        if not bits:
            return state
        keep = tie(keep, *deps)
        send, kept = split_add(line_side(bits[0]), keep, got)
        return kept, swap(send, "seq", bits[0]), bits[1:]

    def halves(*parts):
        rows, columns = parts[0].shape
        return pl.pallas_call(
            halves_kernel,
            in_specs=[pl.BlockSpec(memory_space=pltpu.SMEM)] + [pl.BlockSpec((rows, columns))] * len(parts),
            out_shape=[struct((rows, columns // 2), jnp.bfloat16)] * 2,
            compiler_params=pltpu.CompilerParams(vmem_limit_bytes=VMEM_LIMIT),
            cost_estimate=LIGHT,
        )(side_scalar, *parts)

    def exchange(mine, theirs):
        both = [jnp.where(side == 0, mine, theirs), jnp.where(side == 0, theirs, mine)]
        return joined(*both).astype(jnp.float32)

    act_other1 = beside(act_send1)

    clock = [two2]

    def at(value, *arrived):
        return tie(value, clock[0], *arrived)

    def mark(results):
        clock[0] = results[0] if isinstance(results, (list, tuple)) else results
        return results

    core = lambda value: swap(value, "tp", 1)
    chip = lambda value: swap(value, "tp", 2)

    two_over = mark(add_low(at(two2, act_other0, two_other, ups_other[2]), core(two3)))
    two_own, two_got = core(two1), chip(two_over)
    middle_grads, middle_low, sums_two = mark(
        call(
            middle_back_kernel,
            [rows_wide, rows_low, struct((4, dim), jnp.float32)],
            middle, two0, two_own, two_got, grad_out, at(row(ln2_gain)),
        )
    )
    mid_beside, mid_across = core(middle_low), chip(middle_low)
    low_other0, low_other1 = beside(at(low_send0)), beside(at(low_send1))
    ups = ups_own + full_gather(ups_other, middle_low)
    part_p, clock[0] = weight_grads(places, (ups, (at(act_keep0), act_keep1, act_other0, act_other1)))
    mid_opposite = core(at(mid_across))
    mids_own = (middle_low, mid_beside, mid_across, mid_opposite)

    attended_grads = mark(
        call(attended_grads_kernel, struct(attended.shape, jnp.bfloat16), *mids_own, at(w_out))
    )
    sum_p = group_sum(touch(part_p, mid_beside))
    twos_other = half_gather(at(two_other))
    ones_other = half_gather(at(one_other))
    first_call, last_call = backward_calls(
        queries, keys, values, meta, rows_info, keys_info, norm, attended, attended_grads, heads
    )
    start, delta, *kv_far = mark(first_call(attended_grads))
    mid_other = beside(at(middle_low))
    far_over = mark(add_low(at(kv_far[2], low_other0, low_other1, twos_other[2]), core(kv_far[3])))
    twos = (normed_two, two_beside, two_across, two_opposite) + full_gather(twos_other, far_over)
    far_own, far_got = core(kv_far[1]), chip(far_over)
    query_low, bias_query, *kv_near = mark(last_call(start, delta, far_over))

    one2, one3 = mark(
        call(
            functools.partial(project_kernel, 2, dot_nt), [rows_low] * 2,
            at(query_low, far_got, far_own, mid_other, ones_other[2]), w_query,
        )
    )
    ones = blocks_one + full_gather(ones_other, one2)
    near_over = mark(add_low(at(kv_near[2]), core(kv_near[3])))
    mid_others = mid_other, core(at(mid_other)), chip(at(mid_other))
    near_own, near_got = core(kv_near[1]), chip(near_over)
    far_sum = mark(add_low(at(kv_far[0]), far_own, far_got))
    far_there = swap(far_sum, "seq", seq_count // 2)
    one_over = mark(add_low(at(one2), core(one3)))
    one_got = chip(one_over)
    part = struct((group_rows, heads * head_dim // 2), jnp.bfloat16)
    dq_keep, att_keep, sends = mark(
        pl.pallas_call(
            columns_kernel,
            in_specs=[pl.BlockSpec(memory_space=pltpu.SMEM)] + [pl.BlockSpec(query_low.shape)] * 2,
            out_shape=[part, part, struct(query_low.shape, jnp.bfloat16)],
            compiler_params=pltpu.CompilerParams(vmem_limit_bytes=VMEM_LIMIT),
            cost_estimate=LIGHT,
        )(side_scalar, at(query_low), attended)
    )
    others = beside(sends)
    part_f, clock[0] = weight_grads(places, (twos, (at(low_keep0), low_keep1, low_other0, low_other1)))
    kv_slots, there = mark(add_split(at(kv_near[0], others, mid_others[2]), near_own, near_got, far_there))
    sum_f = group_sum(touch(part_f, far_sum))
    there = swap(there, "seq", seq_bits[-2])
    mid_others = (*mid_others, core(at(mid_others[2])))
    one0, one1 = mark(
        call(functools.partial(project_kernel, 0, dot_nt), [rows_low] * 2, at(query_low), w_query)
    )
    one_own = core(one1)
    width = dq_keep.shape[1]
    part_qo, clock[0] = weight_grads(
        places,
        (ones, (at(dq_keep), others[:, :width])),
        (mids_own + mid_others, (att_keep, others[:, width:])),
    )
    for bit in seq_bits[-3::-1]:
        kv_slots, send = mark(add_split(at(kv_slots), there))
        there = swap(send, "seq", bit)
    kv_low = mark(add_low(at(kv_slots, one_got), there))[0]
    kv_beside, kv_across = core(kv_low), chip(kv_low)
    sum_qo = group_sum(touch(part_qo, kv_low))
    grad_in, sums_one, sums_value = mark(
        call(
            last_kernel,
            [rows_wide, struct((2, dim), jnp.float32), struct((1, head_dim), jnp.float32)],
            hidden_in, one0, one_own, one_got, kv_low, w_kv, middle_grads, at(row(ln1_gain)),
        )
    )

    count = 6 * dim + head_dim
    vectors = [sums_two.reshape(-1), sums_one.reshape(-1), sums_value[0], bias_query[0], (sum_near + sum_far)[0]]
    vectors = jnp.concatenate(vectors).reshape(-1, 128)
    got = swap(vectors, "seq", seq_bits[1])
    kv_group = joined(kv_low, kv_beside, kv_across, core(at(kv_across)))
    kv_other = beside(kv_group)
    mine_p, theirs_p = mark(halves(at(sum_p)))
    theirs_p = beside(theirs_p)
    mlp_over = mark(add_low(at(mlp2), core(at(mlp3))))
    mlp_own, mlp_got = core(at(mlp1)), chip(mlp_over)
    vectors = vectors + at(got)
    got = swap(vectors, "seq", seq_bits[2])
    part_kv = mark(slab_grads(places, ones, (at(kv_group), kv_other), 2 * tp_count))
    got_kv = swap(part_kv, "seq", seq_bits[1])
    vectors = vectors + at(got)
    for bit in seq_bits[2:]:
        part_kv = mark(add_low(at(part_kv), got_kv))
        got_kv = swap(part_kv, "seq", bit)
    for bit in seq_bits[3:]:
        vectors = vectors + swap(vectors, "seq", bit)
    got = swap(vectors, "seq", 1)
    part_kv = mark(add_low(at(part_kv), got_kv))
    got_kv = beside(part_kv)
    layer_out = mark(call(layer_kernel, rows_low, at(middle), mlp0, mlp_own, mlp_got, row(b_proj)))
    vectors = (vectors + at(got)).reshape(-1)
    shared, split = vectors[:count].reshape(-1, 128), vectors[count:]
    got = chip(shared)
    grad_proj = exchange(at(mine_p), theirs_p)
    half_kv = jnp.where(side == 0, jnp.stack([part_kv, got_kv]), jnp.stack([got_kv, part_kv]))
    half_beside, half_across = core(half_kv), chip(half_kv)
    mine_f, theirs_f = mark(halves(tie(sum_f, half_kv)))
    theirs_f = beside(theirs_f)
    shared = shared + at(got)
    got = core(shared)
    half_opposite = core(at(half_across))
    shared = (shared + at(got)).reshape(-1)
    grad_fc = exchange(at(mine_f), theirs_f).T
    quarters = half_kv, half_beside, half_across, half_opposite
    grad_kv = jnp.concatenate(
        [
            jnp.where(tp_index == j, quarters[0], jnp.where(tp_index == j ^ 1, quarters[1], jnp.where(tp_index == j ^ 2, quarters[2], quarters[3])))
            for j in range(tp_count)
        ]
    )
    grad_kv = jnp.swapaxes(grad_kv.astype(jnp.float32), 1, 2).reshape(dim, 2 * head_dim)
    mine_qo, theirs_qo = mark(halves(tie(sum_qo, grad_fc, grad_kv, shared)))
    theirs_qo = beside(theirs_qo)
    grad_query = exchange(mine_qo[:width], theirs_qo[:width]).T
    grad_out_weight = exchange(mine_qo[width:], theirs_qo[width:])
    queries_width = bias_query.shape[1]
    return (
        layer_out,
        grad_in,
        shared[4 * dim : 5 * dim],
        shared[5 * dim : 6 * dim],
        grad_query,
        split[:queries_width],
        grad_kv,
        shared[6 * dim :],
        grad_out_weight,
        shared[3 * dim : 4 * dim],
        shared[dim : 2 * dim],
        shared[2 * dim : 3 * dim],
        grad_fc,
        split[queries_width:],
        grad_proj,
        shared[:dim],
    )


def solution(mesh):
    placed = (
        P(("seq", "tp"), None), P(), P(), P(), P(None, "tp"), P("tp"), P(), P(), P("tp", None),
        P(), P(), P(), P(None, "tp"), P("tp"), P("tp", None), P(), P(("seq", "tp"), None),
    )
    returned = (
        P(("seq", "tp"), None), P(("seq", "tp"), None), P(), P(), P("seq", "tp"), P("tp"), P(), P(),
        P("tp", "seq"), P(), P(), P(), P("seq", "tp"), P("tp"), P("tp", "seq"), P(),
    )
    return jax.shard_map(body, mesh=mesh, in_specs=placed, out_specs=returned, check_vma=False)
```
